32 devices in a mesh: parts: 2 (over y), dp: 4 (over z), fsdp: 4 (over x, core).
Axes of the slice: x: 2, y: 2, z: 4, core: 2. Of those that a mesh axis runs over, the one named last changes fastest.
Arguments:
- hidden: bfloat16 [7168, 2560], P(('parts', 'dp'), 'fsdp'), parts along dimension 0
- lengths: int32 [24], P(('parts', 'dp')), parts along dimension 0, may hold values from 1 to 560, as said below
- mask_pos: int32 [24], P(('parts', 'dp')), parts along dimension 0, may hold values from 0 to 559, as said below
- token_ids: int32 [7168], P(('parts', 'dp')), parts along dimension 0, may hold values from 4 to 23
- assignment: int32 [24], P(('parts', 'dp')), parts along dimension 0, may hold values from 0 to 11, each once
- w_query: bfloat16 [2560, 2560], P('dp', 'fsdp')
- w_key: bfloat16 [2560, 2560], P('dp', 'fsdp')
- w_value: bfloat16 [2560, 2560], P('dp', 'fsdp'), may hold values from -0.5 to 0.5
- w_out: bfloat16 [2560, 2560], P('fsdp', 'dp'), may hold values from -0.125 to 0.125
- embed: bfloat16 [33, 2560], replicated
Outputs:
- states: bfloat16 [7168, 2560], P(('parts', 'dp'), 'fsdp'), parts along dimension 0
- logits: float32 [24, 33], P(('parts', 'dp')), parts along dimension 0
- scored: float32 [24], P(('parts', 'dp')), parts along dimension 0
The draws below stay inside these ranges and needn't reach their ends.
There are 2 independent parts, one for each index of `parts`. The reference program is written for one: setup_inputs(seed, part) draws one part's arguments, and reference() takes and returns one part's arrays. A program takes and returns all parts, laid end to end along the dimension named above; an argument that names none is the same for every part. Nothing has to cross between parts.
Inputs may be any that keep to these rules, and one draw needn't show every extreme that they name: `lengths`: each run of 3 entries belonging to one index of dp sums to 896, and one entry of each run equals 560. `mask_pos`: each entry lies below its own sequence's length.
All inputs are finite; a program needn't handle non-finite values.
Results may differ from the reference program's by a relative error of at most 0.013.
The reference program's roundings to bfloat16 on the way (of `normed`, `value_rows`, `weights`, `context` and `normed_rows`) count: a program that leaves them out, or rounds other values in their place, can miss the bound.
Values may be sent and summed in bfloat16 or wider, within the bound.
No kernel may reach another device: no remote copies, remote signals or barrier semaphores. Data moves between devices by JAX's collectives and lax.ppermute only.
A program may use at most 128 MiB of HBM per device.

```python
import math
import jax
import jax.numpy as jnp
from jax import lax

D = 2560
H = 20
HS = 128
VOCAB = 33
SEQ_G = 3
TOK_G = 896
MOST = 560
TOKENS = 3584
SEQS = 12


def draw_layout(key):
    key_split, key_turn = jax.random.split(key)
    groups = SEQS // SEQ_G
    remainder = TOK_G - MOST
    split_point = jax.random.randint(key_split, (groups,), 1, remainder)
    triple_len = jnp.stack([jnp.full((groups,), MOST, jnp.int32), split_point, remainder - split_point], 1)
    rotation = jax.random.randint(key_turn, (groups,), 0, 3)
    order = (jnp.arange(3)[None, :] + rotation[:, None]) % 3
    return jnp.take_along_axis(triple_len, order, 1).reshape(SEQS).astype(jnp.int32)


def draw_lengths(key, part):
    lengths = draw_layout(key)
    return lengths


def draw_mask_pos(key, part):
    lengths = draw_layout(key)
    key = jax.random.fold_in(key, 5)
    marks = jax.random.randint(key, (SEQS,), 0, lengths).astype(jnp.int32)
    seq_index = jnp.arange(SEQS, dtype=jnp.int32)
    longest = lengths == MOST
    marks = jnp.where(longest & (seq_index < SEQ_G), MOST - 1, marks)
    marks = jnp.where(longest & (seq_index >= SEQ_G) & (seq_index < 2 * SEQ_G), 0, marks)
    return marks.astype(jnp.int32)


def draw_hidden(key, part):
    key = jax.random.fold_in(key, 11)
    key_base = jax.random.fold_in(key, 0)
    key_cols = jax.random.fold_in(key, 2)
    entries = jax.random.normal(key_base, (TOKENS, D), jnp.float32)
    col_factor = jnp.exp(jax.random.uniform(key_cols, (1, D), jnp.float32, math.log(0.5), math.log(2.0)))
    result = entries * col_factor
    return result.astype(jnp.bfloat16)


def draw_w_query(key, part):
    key = jax.random.fold_in(key, 21)
    entries = jax.random.normal(key, (D, H * HS), jnp.float32) / math.sqrt(D)
    return entries.astype(jnp.bfloat16)


def draw_w_key(key, part):
    key = jax.random.fold_in(key, 22)
    entries = jax.random.normal(key, (D, H * HS), jnp.float32) / math.sqrt(D)
    return entries.astype(jnp.bfloat16)


def draw_embed(key, part):
    key = jax.random.fold_in(key, 23)
    entries = jax.random.normal(key, (VOCAB, D), jnp.float32) * 4.0 / math.sqrt(D)
    return entries.astype(jnp.bfloat16)


def set_ends(drawn, rng, low, high):
    extent = drawn.shape
    spot = [jax.random.randint(jax.random.fold_in(rng, axis), (), 0, extent[axis]) for axis in range(len(extent))]
    drawn = drawn.at[tuple(spot)].set(low)
    longest = extent.index(max(extent))
    spot[longest] = (spot[longest] + 1) % extent[longest]
    return drawn.at[tuple(spot)].set(high)


def steps_of(key, shape, pieces, smallest, top_value):
    level, own = 1.0, jax.random.fold_in(key, 6)
    for axis_at, parts in pieces:
        steps = jnp.exp(jax.random.uniform(jax.random.fold_in(own, axis_at), (parts,), jnp.float32, smallest / len(pieces), top_value / len(pieces)))
        level = level * jnp.repeat(steps, shape[axis_at] // parts).reshape([-1 if axis == axis_at else 1 for axis in range(len(shape))])
    return level


def gaussian(own_key, shape, scale, reach, pieces=(), held_as=jnp.bfloat16):
    array = jax.random.normal(own_key, shape, jnp.float32) * scale
    if len(pieces) > 0:
        array = steps_of(own_key, shape, pieces, -0.22, 0.18) * array
    return jnp.clip(array, min=-reach, max=reach).astype(held_as)


def setup_inputs(seed: int = 0, part: int = 0) -> dict:
    key_of = jax.random.split(jax.random.key(seed), 11)
    part_keys = jax.random.split(jax.random.fold_in(key_of[10], part), 11)
    return {
        "hidden": draw_hidden(jax.random.fold_in(jax.random.fold_in(key_of[10], part), 71), part),
        "lengths": draw_lengths(jax.random.fold_in(jax.random.fold_in(key_of[10], part), 71), part),
        "mask_pos": draw_mask_pos(jax.random.fold_in(jax.random.fold_in(key_of[10], part), 71), part),
        "token_ids": set_ends(jax.random.randint(part_keys[3], (TOKENS,), 4, 24), jax.random.fold_in(part_keys[3], 1), 4, 23).astype(jnp.int32),
        "assignment": jax.random.permutation(part_keys[4], SEQS).astype(jnp.int32),
        "w_query": draw_w_query(jax.random.fold_in(key_of[10], 71), part),
        "w_key": draw_w_key(jax.random.fold_in(key_of[10], 71), part),
        "w_value": gaussian(key_of[7], (D, H * HS), (D // 16) ** -0.5, 0.5, ((0, 4), (1, 4))),
        "w_out": gaussian(key_of[8], (H * HS, D), (H * HS) ** -0.5, 0.125, ((0, 4), (1, 4))),
        "embed": draw_embed(jax.random.fold_in(key_of[10], 71), part),
    }


EPSILON = 1e-05

def norm_rows(values):
    average = lax.optimization_barrier(jnp.mean(values, -1, keepdims=True))
    centred = values - average
    spread = lax.optimization_barrier(jnp.mean(centred * centred, -1, keepdims=True))
    return centred * lax.rsqrt(spread + EPSILON)

def rotate(field, position):
    half_width = field.shape[-1] // 2
    frequency = 10000.0 ** (-2.0 * jnp.arange(half_width, dtype=jnp.float32) / field.shape[-1])
    angles = position.astype(jnp.float32)[:, None] * frequency[None, :]
    angles = jnp.concatenate([angles, angles], -1)[:, None, :]
    turned = jnp.concatenate([-field[..., half_width:], field[..., :half_width]], -1)
    return field * jnp.cos(angles) + turned * jnp.sin(angles)

def layout(lengths, count):
    ends = jnp.cumsum(lengths).astype(jnp.int32)
    starts = (ends - lengths).astype(jnp.int32)
    tok_index = jnp.arange(count, dtype=jnp.int32)
    inside = (tok_index[:, None] >= starts[None, :]) & (tok_index[:, None] < ends[None, :])
    labels = jnp.arange(lengths.shape[0], dtype=jnp.int32)
    segment = lax.optimization_barrier(jnp.sum(jnp.where(inside, labels[None, :], 0), 1)).astype(jnp.int32)
    position = (tok_index - lax.optimization_barrier(jnp.sum(jnp.where(inside, starts[None, :], 0), 1))).astype(jnp.int32)
    return (segment, position, starts)

def attend(queries, key_rows, value_rows, same_seq):

    def one_head(triple):
        query_head, key_head, value_head = triple
        scores = jnp.dot(query_head, key_head.T, preferred_element_type=jnp.float32)
        scores = jnp.where(same_seq, scores, -1e+30)
        weights = jax.nn.softmax(scores, -1).astype(jnp.bfloat16)
        return jnp.dot(weights, value_head, preferred_element_type=jnp.float32).astype(jnp.bfloat16)
    stacked = lax.map(one_head, (queries.transpose(1, 0, 2), key_rows.transpose(1, 0, 2), value_rows.transpose(1, 0, 2)))
    return stacked.transpose(1, 0, 2).reshape(queries.shape[0], -1)

def reference(hidden, lengths, mask_pos, token_ids, assignment, w_query, w_key, w_value, w_out, embed):
    groups = SEQS // SEQ_G

    def one_group(bundle):
        block, group_lengths, marks, group_ids = bundle
        segment, position, starts = layout(group_lengths, TOK_G)
        normed = norm_rows(block.astype(jnp.float32)).astype(jnp.bfloat16)
        query_sum = jnp.dot(normed, w_query, preferred_element_type=jnp.float32) * HS ** (-0.5)
        queries = rotate(query_sum.reshape(TOK_G, H, HS), position).astype(jnp.bfloat16)
        key_sum = jnp.dot(normed, w_key, preferred_element_type=jnp.float32)
        key_rows = rotate(key_sum.reshape(TOK_G, H, HS), position).astype(jnp.bfloat16)
        value_rows = jnp.dot(normed, w_value, preferred_element_type=jnp.float32).astype(jnp.bfloat16).reshape(TOK_G, H, HS)
        context = attend(queries, key_rows, value_rows, segment[:, None] == segment[None, :])
        attended = jnp.dot(context, w_out, preferred_element_type=jnp.float32)
        states = (block.astype(jnp.float32) + attended).astype(jnp.bfloat16)
        picked = (starts + marks).astype(jnp.int32)
        return (states, states[picked], group_ids[picked])
    states, masked_rows, masked_ids = lax.map(one_group, (hidden.reshape(groups, TOK_G, D), lengths.reshape(groups, SEQ_G), mask_pos.reshape(groups, SEQ_G), token_ids.reshape(groups, TOK_G)))
    masked_rows = masked_rows.reshape(SEQS, D)
    masked_ids = masked_ids.reshape(SEQS)
    owner_rows = jnp.zeros_like(masked_rows).at[assignment].set(masked_rows)
    owner_ids = jnp.zeros_like(masked_ids).at[assignment].set(masked_ids)
    normed_rows = norm_rows(owner_rows.astype(jnp.float32)).astype(jnp.bfloat16)
    logits = jnp.dot(normed_rows, embed.T, preferred_element_type=jnp.float32)
    target = jnp.take_along_axis(logits, owner_ids[:, None].astype(jnp.int32), 1)[:, 0]
    scored = target - jax.nn.logsumexp(logits, -1)
    return (states.reshape(TOKENS, D), logits, scored)
```

```python
import functools

import jax
import jax.numpy as jnp
from jax import lax
from jax.experimental import pallas as pl
from jax.experimental.pallas import tpu as pltpu
from jax.sharding import PartitionSpec as P

HS = 128
SEQ_G = 3


EPSILON = 1e-05


def norm_rows(values):
    average = jnp.mean(values, -1, keepdims=True)
    centred = values - average
    spread = jnp.mean(centred * centred, -1, keepdims=True)
    return centred * lax.rsqrt(spread + EPSILON)


def rotate(field, position):
    half_width = field.shape[-1] // 2
    frequency = 10000.0 ** (-2.0 * jnp.arange(half_width, dtype=jnp.float32) / field.shape[-1])
    angles = position.astype(jnp.float32)[:, None] * frequency[None, :]
    angles = jnp.concatenate([angles, angles], -1)[:, None, :]
    turned = jnp.concatenate([-field[..., half_width:], field[..., :half_width]], -1)
    return field * jnp.cos(angles) + turned * jnp.sin(angles)


def layout(lengths, count):
    ends = jnp.cumsum(lengths)
    starts = ends - lengths
    tok_index = jnp.arange(count, dtype=jnp.int32)
    inside = (tok_index[:, None] >= starts[None, :]) & (tok_index[:, None] < ends[None, :])
    labels = jnp.arange(lengths.shape[0], dtype=jnp.int32)
    segment = jnp.sum(jnp.where(inside, labels[None, :], 0), 1)
    position = tok_index - jnp.sum(jnp.where(inside, starts[None, :], 0), 1)
    return (segment, position, starts)


def attend(queries, key_rows, value_rows, same_seq):

    def one_head(triple):
        query_head, key_head, value_head = triple
        scores = jnp.dot(query_head, key_head.T, preferred_element_type=jnp.float32)
        scores = jnp.where(same_seq, scores, -1e30)
        weights = jax.nn.softmax(scores, -1).astype(jnp.bfloat16)
        return jnp.dot(weights, value_head, preferred_element_type=jnp.float32).astype(jnp.bfloat16)

    stacked = lax.map(
        one_head,
        (queries.transpose(1, 0, 2), key_rows.transpose(1, 0, 2), value_rows.transpose(1, 0, 2)),
    )
    return stacked.transpose(1, 0, 2).reshape(queries.shape[0], -1)


def target_score(logits, target_ids):
    vocab_index = jnp.arange(logits.shape[1], dtype=jnp.int32)
    target = jnp.sum(jnp.where(vocab_index[None, :] == target_ids[:, None], logits, 0.0), 1)
    return target - jax.nn.logsumexp(logits, -1)


def per_device_any(
    hidden, lengths, mask_pos, token_ids, assignment, w_query, w_key, w_value, w_out, embed
):
    tokens_here = hidden.shape[0]
    gathered = lax.all_gather(hidden, "fsdp", axis=1, tiled=True)
    normed = norm_rows(gathered.astype(jnp.float32)).astype(jnp.bfloat16)
    query_sum = jnp.dot(
        normed,
        lax.all_gather(w_query, "dp", axis=0, tiled=True),
        preferred_element_type=jnp.float32,
    )
    key_sum = jnp.dot(
        normed, lax.all_gather(w_key, "dp", axis=0, tiled=True), preferred_element_type=jnp.float32
    )
    value_sum = jnp.dot(
        normed,
        lax.all_gather(w_value, "dp", axis=0, tiled=True),
        preferred_element_type=jnp.float32,
    )
    heads_here = w_query.shape[1] // HS
    segment, position, starts = layout(lengths, tokens_here)
    queries = rotate(
        (query_sum * HS ** (-0.5)).reshape(tokens_here, heads_here, HS), position
    ).astype(jnp.bfloat16)
    key_rows = rotate(key_sum.reshape(tokens_here, heads_here, HS), position).astype(jnp.bfloat16)
    value_rows = value_sum.astype(jnp.bfloat16).reshape(tokens_here, heads_here, HS)
    context = attend(queries, key_rows, value_rows, segment[:, None] == segment[None, :])
    partials = jnp.dot(
        context, lax.all_gather(w_out, "dp", axis=1, tiled=True), preferred_element_type=jnp.float32
    )
    attended = lax.psum_scatter(
        partials.astype(jnp.bfloat16), "fsdp", scatter_dimension=1, tiled=True
    ).astype(jnp.float32)
    states = (hidden.astype(jnp.float32) + attended).astype(jnp.bfloat16)
    picked = starts + mask_pos
    chosen = jnp.arange(tokens_here, dtype=jnp.int32)[None, :] == picked[:, None]
    local_rows = jnp.dot(
        chosen.astype(jnp.bfloat16), states, preferred_element_type=jnp.float32
    ).astype(jnp.bfloat16)
    local_ids = jnp.sum(jnp.where(chosen, token_ids[None, :], 0), 1)
    row_full = lax.all_gather(local_rows, "fsdp", axis=1, tiled=True)
    owned_slots = lax.axis_index("dp") * SEQ_G + jnp.arange(SEQ_G, dtype=jnp.int32)
    all_rows, all_ids, all_owner = (
        lax.all_gather(row_full, "dp", axis=0, tiled=True),
        lax.all_gather(local_ids, "dp", axis=0, tiled=True),
        lax.all_gather(assignment, "dp", axis=0, tiled=True),
    )
    match_owner = all_owner[None, :] == owned_slots[:, None]
    mine_rows = jnp.dot(
        match_owner.astype(jnp.bfloat16), all_rows, preferred_element_type=jnp.float32
    ).astype(jnp.bfloat16)
    mine_ids = jnp.sum(jnp.where(match_owner, all_ids[None, :], 0), 1).astype(jnp.int32)
    normed_rows = norm_rows(mine_rows.astype(jnp.float32)).astype(jnp.bfloat16)
    logits = jnp.dot(normed_rows, embed.T, preferred_element_type=jnp.float32)
    scored = target_score(logits, mine_ids)
    return (states, logits, scored)

F32 = jnp.float32
BF16 = jnp.bfloat16
VMEM_LIMIT = 48 * 1024 * 1024
SMEM_SPEC = pl.BlockSpec(memory_space=pltpu.SMEM)
ANY_SPEC = pl.BlockSpec(memory_space=pl.ANY)


def params(*semantics):
    return pltpu.CompilerParams(
        vmem_limit_bytes=VMEM_LIMIT, dimension_semantics=semantics or None
    )


def norm_kernel(x_ref, out_ref):
    blocks, _, width = x_ref.shape
    count = blocks * width
    values = [x_ref[b].astype(F32) for b in range(blocks)]
    average = sum(jnp.sum(v, -1, keepdims=True) for v in values) / count
    centred = [v - average for v in values]
    spread = sum(jnp.sum(v * v, -1, keepdims=True) for v in centred) / count
    scale = lax.rsqrt(spread + EPSILON)
    for b in range(blocks):
        out_ref[b] = (centred[b] * scale).astype(BF16)


def norm_blocks(stack, row_block=128):
    blocks, rows, width = stack.shape
    spec = pl.BlockSpec((blocks, row_block, width), lambda i: (0, i, 0))
    return pl.pallas_call(
        norm_kernel,
        grid=(rows // row_block,),
        in_specs=[spec],
        out_specs=spec,
        out_shape=jax.ShapeDtypeStruct(stack.shape, BF16),
        compiler_params=params("arbitrary"),
        cost_estimate=pl.CostEstimate(
            flops=8 * stack.size, bytes_accessed=4 * stack.size, transcendentals=rows
        ),
        name="norm_rows",
    )(stack)


def weight_copies(part, own, pieces, wbuf, sems):
    copies = []
    slot = 0
    if own is not None:
        copies.append([pltpu.make_async_copy(own, wbuf.at[0], sems.at[0])])
        slot = 1
    half = wbuf.shape[1] // 2
    for k, (mine, other) in enumerate(pieces):
        first = pl.multiple_of(part * half, half)
        second = pl.multiple_of((1 - part) * half, half)
        copies.append(
            [
                pltpu.make_async_copy(
                    mine, wbuf.at[slot + k, pl.ds(first, half)], sems.at[slot + 2 * k]
                ),
                pltpu.make_async_copy(
                    other, wbuf.at[slot + k, pl.ds(second, half)], sems.at[slot + 2 * k + 1]
                ),
            ]
        )
    return copies


def project_kernel(scale, rotated, place_ref, x_ref, *refs):
    own, a1, b1, a2, b2, a3, b3 = refs[:7]
    if rotated:
        cos_ref, sin_ref = refs[7:9]
    out_ref, wbuf, sems = refs[-3:]
    copies = weight_copies(place_ref[4], own, ((a1, b1), (a2, b2), (a3, b3)), wbuf, sems)
    first_step = pl.program_id(0) == 0

    @pl.when(first_step)
    def _():
        for group in copies:
            for copy in group:
                copy.start()

    total = None
    for k in range(4):

        @pl.when(first_step)
        def _():
            for copy in copies[k]:
                copy.wait()

        term = jnp.dot(x_ref[place_ref[k]], wbuf[k], preferred_element_type=F32)
        total = term if total is None else total + term
    if scale is not None:
        total = total * scale
    if not rotated:
        out_ref[...] = total.astype(BF16)
        return
    cos, sin = cos_ref[...], sin_ref[...]
    for h in range(total.shape[1] // HS):
        field = total[:, h * HS : (h + 1) * HS]
        turned = pltpu.roll(field, HS // 2, 1)
        out_ref[:, h * HS : (h + 1) * HS] = (field * cos + turned * sin).astype(BF16)


def project(place, normed, own, pieces, turn=None, scale=None, row_block=448):
    blocks, rows, depth = normed.shape
    columns = own.shape[1]
    flat = [ref for pair in pieces for ref in pair]
    in_specs = [SMEM_SPEC, pl.BlockSpec((blocks, row_block, depth), lambda i: (0, i, 0))]
    in_specs += [ANY_SPEC] * 7
    operands = [place, normed, own, *flat]
    if turn is not None:
        in_specs += [pl.BlockSpec((row_block, HS), lambda i: (i, 0))] * 2
        operands += list(turn)
    return pl.pallas_call(
        functools.partial(project_kernel, scale, turn is not None),
        grid=(rows // row_block,),
        in_specs=in_specs,
        out_specs=pl.BlockSpec((row_block, columns), lambda i: (i, 0)),
        out_shape=jax.ShapeDtypeStruct((rows, columns), BF16),
        scratch_shapes=[
            pltpu.VMEM((blocks, depth, columns), BF16),
            pltpu.SemaphoreType.DMA((7,)),
        ],
        compiler_params=params("arbitrary"),
        cost_estimate=pl.CostEstimate(
            flops=2 * rows * blocks * depth * columns,
            bytes_accessed=2 * (normed.size + blocks * depth * columns + rows * columns),
            transcendentals=0,
        ),
        name="project",
    )(*operands)


def attend_kernel(ends_ref, q_ref, k_ref, v_ref, out_ref, *, row_block):
    count = k_ref.shape[0]
    keys, values = k_ref[...], v_ref[...]
    base = pl.program_id(0) * q_ref.shape[0]
    col = lax.broadcasted_iota(jnp.int32, (1, count), 1)
    sequences = ends_ref.shape[0]
    col_label = sum((col >= ends_ref[j]).astype(jnp.int32) for j in range(sequences - 1))
    for r in range(q_ref.shape[0] // row_block):
        span = slice(r * row_block, (r + 1) * row_block)
        row = lax.broadcasted_iota(jnp.int32, (row_block, 1), 0) + (base + r * row_block)
        row_label = sum((row >= ends_ref[j]).astype(jnp.int32) for j in range(sequences - 1))
        scores = lax.dot_general(
            q_ref[span, :], keys, (((1,), (1,)), ((), ())), preferred_element_type=F32
        )
        scores = jnp.where(row_label == col_label, scores, -1e30)
        top = jnp.max(scores, -1, keepdims=True)
        raised = jnp.exp(scores - top)
        weights = raised * (1.0 / jnp.sum(raised, -1, keepdims=True))
        out_ref[span, :] = jnp.dot(
            weights.astype(BF16), values, preferred_element_type=F32
        ).astype(BF16)


def attention(ends, queries, key_rows, value_rows, q_block=448, row_block=224):
    rows, columns = queries.shape
    heads = columns // HS
    return pl.pallas_call(
        functools.partial(attend_kernel, row_block=row_block),
        grid=(rows // q_block, heads),
        in_specs=[
            SMEM_SPEC,
            pl.BlockSpec((q_block, HS), lambda i, h: (i, h)),
            pl.BlockSpec((rows, HS), lambda i, h: (0, h)),
            pl.BlockSpec((rows, HS), lambda i, h: (0, h)),
        ],
        out_specs=pl.BlockSpec((q_block, HS), lambda i, h: (i, h)),
        out_shape=jax.ShapeDtypeStruct((rows, columns), BF16),
        compiler_params=params("arbitrary", "arbitrary"),
        cost_estimate=pl.CostEstimate(
            flops=4 * rows * rows * columns,
            bytes_accessed=8 * rows * columns,
            transcendentals=rows * rows * heads,
        ),
        name="attention",
    )(ends, queries, key_rows, value_rows)


def out_kernel(with_own, pairs, place_ref, x_ref, *refs):
    refs = list(refs)
    own = refs.pop(0) if with_own else None
    pieces = [(refs.pop(0), refs.pop(0)) for _ in range(pairs)]
    shards = pairs + with_own
    outs = [refs.pop(0) for _ in range(shards)]
    wbuf, sems = refs
    copies = weight_copies(place_ref[0], own, pieces, wbuf, sems)
    for group in copies:
        for copy in group:
            copy.start()
    context = x_ref[...]
    for k in range(shards):
        for copy in copies[k]:
            copy.wait()
        outs[k][...] = jnp.dot(context, wbuf[k], preferred_element_type=F32).astype(
            outs[k].dtype
        )


def out_project(place, context, own, pieces, dtype):
    rows, depth = context.shape
    half = rows // 2
    columns = pieces[0][0].shape[1]
    flat = [ref for pair in pieces for ref in pair]
    with_own = own is not None
    operands = ([own] if with_own else []) + flat
    shards = len(pieces) + with_own
    return pl.pallas_call(
        functools.partial(out_kernel, int(with_own), len(pieces)),
        grid_spec=pltpu.PrefetchScalarGridSpec(
            num_scalar_prefetch=1,
            grid=(1,),
            in_specs=[pl.BlockSpec((half, depth), lambda i, place: (place[1], 0))]
            + [ANY_SPEC] * len(operands),
            out_specs=[pl.BlockSpec((half, columns), lambda i, place: (0, 0))] * shards,
            scratch_shapes=[
                pltpu.VMEM((shards, depth, columns), BF16),
                pltpu.SemaphoreType.DMA((2 * len(pieces) + with_own,)),
            ],
        ),
        out_shape=[jax.ShapeDtypeStruct((half, columns), dtype)] * shards,
        compiler_params=params("arbitrary"),
        cost_estimate=pl.CostEstimate(
            flops=2 * shards * half * depth * columns,
            bytes_accessed=2 * (half * depth + shards * (depth + 2 * half) * columns),
            transcendentals=0,
        ),
        name="out_project",
    )(place, context, *operands)


def tie(value, *earlier):
    return lax.optimization_barrier((value, *earlier))[0]


def gather_weights(weights, dp):
    part = lax.axis_index("parts")
    ring = lambda x, step: lax.ppermute(x, "dp", [(i, (i + step) % dp) for i in range(dp)])
    swap = lambda x: lax.ppermute(x, "parts", [(0, 1), (1, 0)])
    along, across = [], []
    result = []
    for weight in weights:
        half = weight.shape[0] // 2
        mine = lax.dynamic_slice_in_dim(weight, part * half, half, 0)
        first = len(along)
        for step in range(3):
            i = len(along)
            source, shift = ((mine, 1), (mine, -1), (along[first] if step == 2 else None, 1))[step]
            if i >= 2:
                source = tie(source, along[i - 2])
            along.append(ring(source, shift))
            source = along[i]
            if i >= 2:
                source = tie(source, across[i - 2])
            across.append(swap(source))
        order = (first, first + 2, first + 1)
        result.append([(along[i], across[i]) for i in order])
    return result


def per_device(
    hidden, lengths, mask_pos, token_ids, assignment, w_query, w_key, w_value, w_out, embed
):
    dp, fsdp = 4, 4
    rows, width = hidden.shape
    half = rows // 2
    sequences = lengths.shape[0]
    part = lax.axis_index("parts")
    group = lax.axis_index("dp")
    column = lax.axis_index("fsdp")
    core = column % 2
    ring_order = [lax.rem(group + dp - k, dp) for k in range(dp)]
    place = jnp.stack(ring_order + [part]).astype(jnp.int32)

    stack = lax.all_gather(hidden, "fsdp", axis=0, tiled=False)
    key_in, query_in, value_in, out_in = gather_weights((w_key, w_query, w_value, w_out), dp)

    segment, position, starts = layout(lengths, rows)
    half_width = HS // 2
    frequency = 10000.0 ** (-2.0 * jnp.arange(half_width, dtype=F32) / HS)
    angles = position.astype(F32)[:, None] * frequency[None, :]
    sine, cosine = jnp.sin(angles), jnp.cos(angles)
    turn = (jnp.concatenate([cosine, cosine], -1), jnp.concatenate([-sine, sine], -1))
    picked = starts + mask_pos
    chosen = jnp.arange(rows, dtype=jnp.int32)[None, :] == picked[:, None]
    local_ids = jnp.sum(jnp.where(chosen, token_ids[None, :], 0), 1)

    normed = norm_blocks(stack)
    key_rows = project(place, normed, w_key, key_in, turn)
    queries = project(place, normed, w_query, query_in, turn, HS ** (-0.5))
    value_rows = project(place, normed, w_value, value_in)
    context = attention(jnp.cumsum(lengths), queries, key_rows, value_rows)

    swap_core = lambda x: lax.ppermute(x, "fsdp", [(i, i ^ 1) for i in range(fsdp)])
    keep_place = jnp.stack([part, core]).astype(jnp.int32)
    send_place = jnp.stack([part, 1 - core]).astype(jnp.int32)
    early = [out_in[0], out_in[2]]
    sent = out_project(send_place, context, w_out, early, BF16)
    sent_late = lambda c: out_project(send_place, c, None, [out_in[1]], BF16)
    arrived = [swap_core(x) for x in sent]
    kept = out_project(keep_place, context, w_out, early, F32)
    late = sent_late(context)
    arrived_late = swap_core(late[0])
    kept_late = out_project(keep_place, context, None, [out_in[1]], F32)

    def cross(k, value):
        pairs = []
        for z in range(dp):
            target = ((z - k) % dp) // 2
            for c in range(2):
                pairs.append((z * fsdp + (1 - target) * 2 + c, z * fsdp + target * 2 + c))
        return lax.ppermute(value, ("dp", "fsdp"), pairs)

    chip, crossed = {}, {}
    for k, keep, come in (
        (0, kept[0], arrived[0]),
        (1, kept[1], arrived[1]),
        (3, kept[2], arrived[2]),
        (2, kept_late[0], arrived_late),
    ):
        chip[k] = keep + come.astype(F32)
        crossed[k] = cross(k, chip[k].astype(BF16)).astype(F32)

    def block_rows(index):
        total = stack_half(index)
        for k in range(dp):
            total += jnp.where(ring_order[k] == index, chip[k] + crossed[k], 0.0)
        return total.astype(BF16)

    def stack_half(index):
        return lax.dynamic_slice(stack, (index, core * half, 0), (1, half, width))[0].astype(F32)

    other_rows = swap_core(block_rows(column ^ 1))
    my_rows = block_rows(column)
    states = jnp.where(
        core == 0,
        jnp.concatenate([my_rows, other_rows], 0),
        jnp.concatenate([other_rows, my_rows], 0),
    )

    one_hot = chosen.astype(BF16)
    context_rows = jnp.dot(one_hot, context, preferred_element_type=F32).astype(BF16)
    hidden_rows = jnp.einsum("sr,brw->bsw", one_hot, stack, preferred_element_type=F32)
    piece_height = width // 2
    by_ring = [jnp.dot(context_rows, w_out, preferred_element_type=F32)]
    mine_part = lax.dynamic_slice_in_dim(context_rows, part * piece_height, piece_height, 1)
    other_part = lax.dynamic_slice_in_dim(context_rows, (1 - part) * piece_height, piece_height, 1)
    for mine, other in out_in:
        by_ring.append(
            jnp.dot(mine_part, mine, preferred_element_type=F32)
            + jnp.dot(other_part, other, preferred_element_type=F32)
        )
    by_ring = jnp.stack(by_ring)
    row_sum = jnp.stack(
        [
            lax.dynamic_index_in_dim(by_ring, lax.rem(group + dp - b, dp), 0, keepdims=False)
            for b in range(dp)
        ]
    )
    row_sum = row_sum + swap_core(row_sum)
    row_sum = row_sum + lax.ppermute(row_sum, "fsdp", [(i, i ^ 2) for i in range(fsdp)])
    full_rows = (hidden_rows + row_sum).astype(BF16)
    full_rows = full_rows.transpose(1, 0, 2).reshape(sequences, dp * width)
    extra = jnp.stack([local_ids, assignment], 1).astype(BF16)
    extra = jnp.pad(extra, ((0, 0), (0, HS - 2)))
    packet = jnp.concatenate([full_rows, extra], 1)
    packets = [packet] + [
        lax.ppermute(packet, "dp", [(i, (i + s) % dp) for i in range(dp)]) for s in range(1, dp)
    ]
    packets = jnp.concatenate(packets, 0)
    all_rows = packets[:, : dp * width]
    all_ids = packets[:, dp * width].astype(jnp.int32)
    all_owner = packets[:, dp * width + 1].astype(jnp.int32)
    owned = group * sequences + jnp.arange(sequences, dtype=jnp.int32)
    match = all_owner[None, :] == owned[:, None]
    mine_rows = jnp.dot(match.astype(BF16), all_rows, preferred_element_type=F32)
    mine_ids = jnp.sum(jnp.where(match, all_ids[None, :], 0), 1).astype(jnp.int32)
    normed_rows = norm_rows(mine_rows).astype(BF16)
    logits = jnp.dot(normed_rows, embed.T, preferred_element_type=F32)
    scored = target_score(logits, mine_ids)
    return (states, logits, scored)


def ring_fits(mesh):
    return (mesh.shape["parts"], mesh.shape["dp"], mesh.shape["fsdp"]) == (2, 4, 4)


def solution(mesh):
    return jax.shard_map(
        per_device if ring_fits(mesh) else per_device_any,
        mesh=mesh,
        in_specs=(
            P(("parts", "dp"), "fsdp"),
            P(("parts", "dp")),
            P(("parts", "dp")),
            P(("parts", "dp")),
            P(("parts", "dp")),
            P("dp", "fsdp"),
            P("dp", "fsdp"),
            P("dp", "fsdp"),
            P("fsdp", "dp"),
            P(),
        ),
        out_specs=(P(("parts", "dp"), "fsdp"), P(("parts", "dp"), None), P(("parts", "dp"))),
        check_vma=False,
    )
```

```python
import functools

import jax
import jax.numpy as jnp
from jax import lax
from jax.experimental import pallas as pl
from jax.experimental.pallas import tpu as pltpu
from jax.sharding import PartitionSpec as P

HS = 128
SEQ_G = 3


EPSILON = 1e-05


def norm_rows(values):
    average = jnp.mean(values, -1, keepdims=True)
    centred = values - average
    spread = jnp.mean(centred * centred, -1, keepdims=True)
    return centred * lax.rsqrt(spread + EPSILON)


def rotate(field, position):
    half_width = field.shape[-1] // 2
    frequency = 10000.0 ** (-2.0 * jnp.arange(half_width, dtype=jnp.float32) / field.shape[-1])
    angles = position.astype(jnp.float32)[:, None] * frequency[None, :]
    angles = jnp.concatenate([angles, angles], -1)[:, None, :]
    turned = jnp.concatenate([-field[..., half_width:], field[..., :half_width]], -1)
    return field * jnp.cos(angles) + turned * jnp.sin(angles)


def layout(lengths, count):
    ends = jnp.cumsum(lengths)
    starts = ends - lengths
    tok_index = jnp.arange(count, dtype=jnp.int32)
    inside = (tok_index[:, None] >= starts[None, :]) & (tok_index[:, None] < ends[None, :])
    labels = jnp.arange(lengths.shape[0], dtype=jnp.int32)
    segment = jnp.sum(jnp.where(inside, labels[None, :], 0), 1)
    position = tok_index - jnp.sum(jnp.where(inside, starts[None, :], 0), 1)
    return (segment, position, starts)


def attend(queries, key_rows, value_rows, same_seq):

    def one_head(triple):
        query_head, key_head, value_head = triple
        scores = jnp.dot(query_head, key_head.T, preferred_element_type=jnp.float32)
        scores = jnp.where(same_seq, scores, -1e30)
        weights = jax.nn.softmax(scores, -1).astype(jnp.bfloat16)
        return jnp.dot(weights, value_head, preferred_element_type=jnp.float32).astype(jnp.bfloat16)

    stacked = lax.map(
        one_head,
        (queries.transpose(1, 0, 2), key_rows.transpose(1, 0, 2), value_rows.transpose(1, 0, 2)),
    )
    return stacked.transpose(1, 0, 2).reshape(queries.shape[0], -1)


def target_score(logits, target_ids):
    vocab_index = jnp.arange(logits.shape[1], dtype=jnp.int32)
    target = jnp.sum(jnp.where(vocab_index[None, :] == target_ids[:, None], logits, 0.0), 1)
    return target - jax.nn.logsumexp(logits, -1)


def per_device_any(
    hidden, lengths, mask_pos, token_ids, assignment, w_query, w_key, w_value, w_out, embed
):
    tokens_here = hidden.shape[0]
    gathered = lax.all_gather(hidden, "fsdp", axis=1, tiled=True)
    normed = norm_rows(gathered.astype(jnp.float32)).astype(jnp.bfloat16)
    query_sum = jnp.dot(
        normed,
        lax.all_gather(w_query, "dp", axis=0, tiled=True),
        preferred_element_type=jnp.float32,
    )
    key_sum = jnp.dot(
        normed, lax.all_gather(w_key, "dp", axis=0, tiled=True), preferred_element_type=jnp.float32
    )
    value_sum = jnp.dot(
        normed,
        lax.all_gather(w_value, "dp", axis=0, tiled=True),
        preferred_element_type=jnp.float32,
    )
    heads_here = w_query.shape[1] // HS
    segment, position, starts = layout(lengths, tokens_here)
    queries = rotate(
        (query_sum * HS ** (-0.5)).reshape(tokens_here, heads_here, HS), position
    ).astype(jnp.bfloat16)
    key_rows = rotate(key_sum.reshape(tokens_here, heads_here, HS), position).astype(jnp.bfloat16)
    value_rows = value_sum.astype(jnp.bfloat16).reshape(tokens_here, heads_here, HS)
    context = attend(queries, key_rows, value_rows, segment[:, None] == segment[None, :])
    partials = jnp.dot(
        context, lax.all_gather(w_out, "dp", axis=1, tiled=True), preferred_element_type=jnp.float32
    )
    attended = lax.psum_scatter(
        partials.astype(jnp.bfloat16), "fsdp", scatter_dimension=1, tiled=True
    ).astype(jnp.float32)
    states = (hidden.astype(jnp.float32) + attended).astype(jnp.bfloat16)
    picked = starts + mask_pos
    chosen = jnp.arange(tokens_here, dtype=jnp.int32)[None, :] == picked[:, None]
    local_rows = jnp.dot(
        chosen.astype(jnp.bfloat16), states, preferred_element_type=jnp.float32
    ).astype(jnp.bfloat16)
    local_ids = jnp.sum(jnp.where(chosen, token_ids[None, :], 0), 1)
    row_full = lax.all_gather(local_rows, "fsdp", axis=1, tiled=True)
    owned_slots = lax.axis_index("dp") * SEQ_G + jnp.arange(SEQ_G, dtype=jnp.int32)
    all_rows, all_ids, all_owner = (
        lax.all_gather(row_full, "dp", axis=0, tiled=True),
        lax.all_gather(local_ids, "dp", axis=0, tiled=True),
        lax.all_gather(assignment, "dp", axis=0, tiled=True),
    )
    match_owner = all_owner[None, :] == owned_slots[:, None]
    mine_rows = jnp.dot(
        match_owner.astype(jnp.bfloat16), all_rows, preferred_element_type=jnp.float32
    ).astype(jnp.bfloat16)
    mine_ids = jnp.sum(jnp.where(match_owner, all_ids[None, :], 0), 1).astype(jnp.int32)
    normed_rows = norm_rows(mine_rows.astype(jnp.float32)).astype(jnp.bfloat16)
    logits = jnp.dot(normed_rows, embed.T, preferred_element_type=jnp.float32)
    scored = target_score(logits, mine_ids)
    return (states, logits, scored)

F32 = jnp.float32
BF16 = jnp.bfloat16
VMEM_LIMIT = 60 * 1024 * 1024
SMEM_SPEC = pl.BlockSpec(memory_space=pltpu.SMEM)
HBM_SPEC = pl.BlockSpec(memory_space=pltpu.HBM)


def params(*semantics):
    return pltpu.CompilerParams(
        vmem_limit_bytes=VMEM_LIMIT, dimension_semantics=semantics or None
    )


def norm_kernel(x_ref, out_ref):
    blocks, _, width = x_ref.shape
    count = blocks * width
    values = [x_ref[b].astype(F32) for b in range(blocks)]
    average = sum(jnp.sum(v, -1, keepdims=True) for v in values) / count
    centred = [v - average for v in values]
    spread = sum(jnp.sum(v * v, -1, keepdims=True) for v in centred) / count
    scale = lax.rsqrt(spread + EPSILON)
    for b in range(blocks):
        out_ref[:, b * width : (b + 1) * width] = (centred[b] * scale).astype(BF16)


def norm_blocks(stack, row_block=224):
    blocks, rows, width = stack.shape
    return pl.pallas_call(
        norm_kernel,
        grid=(rows // row_block,),
        in_specs=[pl.BlockSpec((blocks, row_block, width), lambda i: (0, i, 0))],
        out_specs=pl.BlockSpec((row_block, blocks * width), lambda i: (i, 0)),
        out_shape=jax.ShapeDtypeStruct((rows, blocks * width), BF16),
        compiler_params=params("arbitrary"),
        cost_estimate=pl.CostEstimate(
            flops=8 * stack.size, bytes_accessed=4 * stack.size, transcendentals=rows
        ),
        name="norm_rows",
    )(stack)


def shard_parts(part, shard, half):
    if len(shard) == 2:
        mine, other = shard
        return [
            (mine, pl.multiple_of(part * half, half)),
            (other, pl.multiple_of((1 - part) * half, half)),
        ]
    return [(shard[0].at[pl.ds(j * half, half)], j * half) for j in range(2)]


def take_shards(refs, lengths):
    return [tuple(refs.pop(0) for _ in range(n)) for n in lengths]


def project_kernel(scale, rotated, lengths, place_ref, x_ref, *refs):
    refs = list(refs)
    shards = take_shards(refs, lengths)
    if rotated:
        cos, sin = refs.pop(0)[...], refs.pop(0)[...]
    out_ref, wbuf, sems = refs
    depth, width = shards[0][0].shape
    half = depth // 2

    @pl.when(pl.program_id(0) == 0)
    def _():
        copies = []
        for k, shard in enumerate(shards):
            for j, (source, row) in enumerate(shard_parts(place_ref[0], shard, half)):
                row = pl.multiple_of(place_ref[1 + k] * depth + row, half)
                copies.append(
                    pltpu.make_async_copy(source, wbuf.at[pl.ds(row, half)], sems.at[k, j])
                )
        for copy in copies:
            copy.start()
        for copy in copies:
            copy.wait()

    total = jnp.dot(x_ref[...], wbuf[...], preferred_element_type=F32)
    if not rotated:
        out_ref[...] = total.astype(BF16)
        return
    if scale is not None:
        total = total * scale
    for h in range(width // HS):
        field = total[:, h * HS : (h + 1) * HS]
        turned = pltpu.roll(field, HS // 2, 1)
        out_ref[:, h * HS : (h + 1) * HS] = (field * cos + turned * sin).astype(BF16)


def project(place, normed, shards, scale=None, turn=(), row_block=448):
    rows, features = normed.shape
    width = shards[0][0].shape[1]
    flat = [ref for shard in shards for ref in shard]
    in_specs = [SMEM_SPEC, pl.BlockSpec((row_block, features), lambda i: (i, 0))]
    in_specs += [HBM_SPEC] * len(flat)
    in_specs += [pl.BlockSpec((row_block, HS), lambda i: (i, 0)) for _ in turn]
    return pl.pallas_call(
        functools.partial(
            project_kernel, scale, bool(turn), [len(shard) for shard in shards]
        ),
        grid=(rows // row_block,),
        in_specs=in_specs,
        out_specs=pl.BlockSpec((row_block, width), lambda i: (i, 0)),
        out_shape=jax.ShapeDtypeStruct((rows, width), BF16),
        scratch_shapes=[
            pltpu.VMEM((features, width), BF16),
            pltpu.SemaphoreType.DMA((4, 2)),
        ],
        compiler_params=params("arbitrary"),
        cost_estimate=pl.CostEstimate(
            flops=2 * rows * features * width,
            bytes_accessed=2 * (normed.size + (features + rows) * width),
            transcendentals=0,
        ),
        name="project",
    )(place, normed, *flat, *turn)


def attend_kernel(place_ref, ends_ref, q_ref, k_ref, v_ref, out_ref, *, row_block):
    count = k_ref.shape[0]
    keys, values = k_ref[...], v_ref[...]
    base = place_ref[1] * q_ref.shape[0]
    col = lax.broadcasted_iota(jnp.int32, (1, count), 1)
    sequences = ends_ref.shape[0]
    col_label = sum((col >= ends_ref[j]).astype(jnp.int32) for j in range(sequences - 1))
    for r in range(q_ref.shape[0] // row_block):
        span = slice(r * row_block, (r + 1) * row_block)
        row = lax.broadcasted_iota(jnp.int32, (row_block, 1), 0) + (base + r * row_block)
        row_label = sum((row >= ends_ref[j]).astype(jnp.int32) for j in range(sequences - 1))
        scores = lax.dot_general(
            q_ref[span, :], keys, (((1,), (1,)), ((), ())), preferred_element_type=F32
        )
        scores = jnp.where(row_label == col_label, scores, -1e30)
        top = jnp.max(scores, -1, keepdims=True)
        raised = jnp.exp(scores - top)
        weights = raised * (1.0 / jnp.sum(raised, -1, keepdims=True))
        out_ref[span, :] = jnp.dot(
            weights.astype(BF16), values, preferred_element_type=F32
        ).astype(BF16)


def attention(place, ends, queries, key_rows, value_rows, row_block=224):
    rows, columns = queries.shape
    half = rows // 2
    heads = columns // HS
    return pl.pallas_call(
        functools.partial(attend_kernel, row_block=row_block),
        grid_spec=pltpu.PrefetchScalarGridSpec(
            num_scalar_prefetch=2,
            grid=(heads,),
            in_specs=[
                pl.BlockSpec((half, HS), lambda h, place, ends: (place[1], h)),
                pl.BlockSpec((rows, HS), lambda h, place, ends: (0, h)),
                pl.BlockSpec((rows, HS), lambda h, place, ends: (0, h)),
            ],
            out_specs=pl.BlockSpec((half, HS), lambda h, place, ends: (0, h)),
        ),
        out_shape=jax.ShapeDtypeStruct((half, columns), BF16),
        compiler_params=params("arbitrary"),
        cost_estimate=pl.CostEstimate(
            flops=4 * half * rows * columns,
            bytes_accessed=6 * rows * columns,
            transcendentals=half * rows * heads,
        ),
        name="attention",
    )(place, ends, queries, key_rows, value_rows)


def out_kernel(adding, lengths, place_ref, *refs):
    refs = list(refs)
    if adding:
        x_ref, come_ref = refs.pop(0), refs.pop(0)
    else:
        picked_ref, x_ref, kept_ref = refs.pop(0), refs.pop(0), refs.pop(0)
    shards = take_shards(refs, lengths)
    out_ref = refs.pop(0)
    if not adding:
        rows_ref, marked = refs.pop(0), refs.pop()
    wbuf, sems = refs
    block = pl.program_id(0)
    half = wbuf.shape[1] // 2
    part, core, column = place_ref[0], place_ref[5], place_ref[6]

    @pl.when(block == 0)
    def _():
        for k, shard in enumerate(shards):
            spot = place_ref[1 + k]
            for j, (source, row) in enumerate(shard_parts(part, shard, half)):
                pltpu.make_async_copy(
                    source, wbuf.at[spot, pl.ds(row, half)], sems.at[spot, j]
                ).start()
        if not adding:
            size = x_ref.shape[0]
            slot = lax.broadcasted_iota(jnp.int32, (marked.shape[0], size), 0)
            row = lax.broadcasted_iota(jnp.int32, (marked.shape[0], size), 1)
            total = None
            for ref, base in ((x_ref, (1 - core) * size), (kept_ref, core * size)):
                hit = sum(
                    ((slot == j) & (row + base == picked_ref[j])).astype(F32)
                    for j in range(picked_ref.shape[0])
                )
                term = jnp.dot(hit.astype(BF16), ref[...], preferred_element_type=F32)
                total = term if total is None else total + term
            marked[...] = total.astype(BF16)

    for j in range(2):
        pltpu.make_async_copy(
            shards[0][0].at[pl.ds(0, half)],
            wbuf.at[block, pl.ds(j * half, half)],
            sems.at[block, j],
        ).wait()
    total = jnp.dot(x_ref[...], wbuf[block], preferred_element_type=F32)
    if adding:
        total = total + come_ref[...].astype(F32)
    else:
        rows_ref[block ^ column] = jnp.dot(
            marked[...], wbuf[block], preferred_element_type=F32
        )
    out_ref[...] = total.astype(BF16)


def out_project(place, context, shards, come=None, picked=None, kept=None):
    half, depth = context.shape
    width = shards[0][0].shape[1]
    flat = [ref for shard in shards for ref in shard]
    adding = come is not None
    whole = pl.BlockSpec((half, depth), lambda j: (0, 0))
    if adding:
        operands = [place, context, come]
        in_specs = [SMEM_SPEC, whole]
        in_specs += [pl.BlockSpec((None, half, width), lambda j: (j ^ 1, 0, 0))]
    else:
        operands = [place, picked, context, kept]
        in_specs = [SMEM_SPEC, SMEM_SPEC, whole, whole]
    out_specs = [pl.BlockSpec((None, half, width), lambda j: (j, 0, 0))]
    out_shape = [jax.ShapeDtypeStruct((4, half, width), BF16)]
    scratch = [pltpu.VMEM((4, depth, width), BF16), pltpu.SemaphoreType.DMA((4, 2))]
    if not adding:
        out_specs.append(pl.BlockSpec((4, 8, width), lambda j: (0, 0, 0)))
        out_shape.append(jax.ShapeDtypeStruct((4, 8, width), F32))
        scratch.append(pltpu.VMEM((8, depth), BF16))
    return pl.pallas_call(
        functools.partial(out_kernel, adding, [len(shard) for shard in shards]),
        grid=(4,),
        in_specs=in_specs + [HBM_SPEC] * len(flat),
        out_specs=out_specs,
        out_shape=out_shape,
        scratch_shapes=scratch,
        compiler_params=params("arbitrary"),
        cost_estimate=pl.CostEstimate(
            flops=8 * half * depth * width,
            bytes_accessed=2 * (half * depth + 4 * (depth + (1 + adding) * half) * width),
            transcendentals=0,
        ),
        name="out_project",
    )(*operands, *flat)


def tie(value, *earlier):
    return lax.optimization_barrier((value, *earlier))[0]


class WeightRing:
    def __init__(self, dp):
        self.dp = dp
        self.part = lax.axis_index("parts")
        self.along, self.across, self.shards = [], [], []

    def ring(self, value, step):
        return lax.ppermute(value, "dp", [(i, (i + step) % self.dp) for i in range(self.dp)])

    def step(self, value, step, before=(), before_swap=(), gather=False):
        i = len(self.along)
        waits = list(before) + self.along[i - 2 : i - 1] if i >= 2 else list(before)
        self.along.append(self.ring(tie(value, *waits), step))
        if gather:
            whole = lax.all_gather(self.along[i], "parts", axis=0, tiled=True)
            self.shards.append((whole,))
            return
        waits = self.across[-2:-1]
        self.across.append(
            lax.ppermute(tie(self.along[i], *waits, *before_swap), "parts", [(0, 1), (1, 0)])
        )
        self.shards.append((self.along[i], self.across[-1]))

    def half(self, weight):
        size = weight.shape[0] // 2
        return lax.dynamic_slice_in_dim(weight, self.part * size, size, 0)

    def pieces(self, group):
        first = 3 * group
        return [self.shards[i] for i in (first, first + 2, first + 1)]


def per_device(
    hidden, lengths, mask_pos, token_ids, assignment, w_query, w_key, w_value, w_out, embed
):
    dp, fsdp = 4, 4
    rows, width = hidden.shape
    half = rows // 2
    sequences = lengths.shape[0]
    part = lax.axis_index("parts")
    group = lax.axis_index("dp")
    column = lax.axis_index("fsdp")
    core = column % 2
    ring_order = [lax.rem(group + dp - k, dp) for k in range(dp)]
    place = jnp.stack([part] + ring_order).astype(jnp.int32)
    stack = lax.all_gather(hidden, "fsdp", axis=0, tiled=False)
    segment, position, starts = layout(lengths, rows)
    half_width = HS // 2
    frequency = 10000.0 ** (-2.0 * jnp.arange(half_width, dtype=F32) / HS)
    angles = position.astype(F32)[:, None] * frequency[None, :]
    sine, cosine = jnp.sin(angles), jnp.cos(angles)
    turn = (jnp.concatenate([cosine, cosine], -1), jnp.concatenate([-sine, sine], -1))
    picked = starts + mask_pos
    chosen = jnp.arange(rows, dtype=jnp.int32)[None, :] == picked[:, None]
    local_ids = jnp.sum(jnp.where(chosen, token_ids[None, :], 0), 1)

    ends = jnp.cumsum(lengths)
    keep_place = jnp.stack([part, core]).astype(jnp.int32)
    send_place = jnp.stack([part, 1 - core]).astype(jnp.int32)
    out_place = jnp.stack([part] + [s ^ column for s in ring_order] + [core, column]).astype(jnp.int32)

    def swap_by(value, mask):
        return lax.ppermute(value, "fsdp", [(i, i ^ mask) for i in range(fsdp)])

    one_hot = chosen.astype(BF16)
    hidden_rows = jnp.einsum("sr,brw->bsw", one_hot, stack, preferred_element_type=F32)
    hidden_rows = jnp.pad(hidden_rows, ((0, 0), (0, 8 - sequences), (0, 0)))
    extra = jnp.stack([local_ids, assignment], 1).astype(BF16)
    extra = jnp.pad(extra, ((0, 8 - sequences), (0, width - 2)))[None]

    ring = WeightRing(dp)
    mine = ring.half(w_key)
    ring.step(mine, 1)
    ring.step(mine, -1)
    ring.step(ring.along[0], 1)
    mine = ring.half(w_query)
    ring.step(mine, 1)
    ring.step(mine, -1)
    normed = norm_blocks(stack)
    ring.step(ring.along[3], 1, before=[normed])
    key_rows = project(place, normed, [(w_key,), *ring.pieces(0)], None, turn)
    mine = ring.half(w_value)
    ring.step(mine, 1, before=[key_rows])
    ring.step(mine, -1)
    ring.step(ring.along[6], 1)
    queries = project(place, normed, [(w_query,), *ring.pieces(1)], HS ** (-0.5), turn)
    mine = ring.half(w_out)
    ring.step(mine, 1, before=[queries])
    value_rows = project(place, normed, [(w_value,), *ring.pieces(2)])
    ring.step(mine, -1, before_swap=[value_rows])
    context_sent = attention(send_place, ends, queries, key_rows, value_rows)
    last_along = ring.ring(tie(ring.along[9], ring.along[9]), 1)
    last_other = ring.ring(tie(ring.across[-2], ring.along[10], context_sent), 1)
    out_in = [(w_out,), ring.shards[9], (last_along, last_other), ring.shards[10]]
    context_kept = attention(keep_place, ends, queries, key_rows, tie(value_rows, context_sent))

    sent, row_sum = out_project(out_place, context_sent, out_in, None, picked, context_kept)
    arrived = swap_by(sent, 1)

    row_sum = row_sum + sum(swap_by(row_sum, mask) for mask in range(1, fsdp))
    full_rows = (hidden_rows + row_sum).astype(BF16)
    packet = jnp.concatenate([full_rows, extra], 0)

    (chip,) = out_project(out_place, tie(context_kept, packet), out_in, arrived)
    crossed = swap_by(chip[2:], 2)

    packets = [packet] + [ring.ring(packet, shift) for shift in range(1, dp)]
    packets = jnp.stack(packets)[:, :, :sequences]
    all_rows = packets[:, :dp].transpose(0, 2, 1, 3).reshape(dp * sequences, dp * width)
    all_ids = packets[:, dp, :, 0].reshape(-1).astype(jnp.int32)
    all_owner = packets[:, dp, :, 1].reshape(-1).astype(jnp.int32)
    owned = group * sequences + jnp.arange(sequences, dtype=jnp.int32)
    match = all_owner[None, :] == owned[:, None]
    mine_rows = jnp.dot(match.astype(BF16), all_rows, preferred_element_type=F32)
    mine_ids = jnp.sum(jnp.where(match, all_ids[None, :], 0), 1).astype(jnp.int32)
    normed_rows = norm_rows(mine_rows).astype(BF16)
    logits = jnp.dot(normed_rows, embed.T, preferred_element_type=F32)
    scored = target_score(logits, mine_ids)

    def block_rows(index, place_in_chip):
        before = lax.dynamic_slice(stack, (index, core * half, 0), (1, half, width))[0]
        summed = chip[place_in_chip].astype(F32) + crossed[place_in_chip].astype(F32)
        return (before.astype(F32) + summed).astype(BF16)

    other_rows = swap_by(block_rows(column ^ 1, 1), 1)
    own_rows = block_rows(column, 0)
    states = jnp.where(
        core == 0,
        jnp.concatenate([own_rows, other_rows], 0),
        jnp.concatenate([other_rows, own_rows], 0),
    )
    return (states, logits, scored)


def ring_fits(mesh):
    return (mesh.shape["parts"], mesh.shape["dp"], mesh.shape["fsdp"]) == (2, 4, 4)


def solution(mesh):
    return jax.shard_map(
        per_device if ring_fits(mesh) else per_device_any,
        mesh=mesh,
        in_specs=(
            P(("parts", "dp"), "fsdp"),
            P(("parts", "dp")),
            P(("parts", "dp")),
            P(("parts", "dp")),
            P(("parts", "dp")),
            P("dp", "fsdp"),
            P("dp", "fsdp"),
            P("dp", "fsdp"),
            P("fsdp", "dp"),
            P(),
        ),
        out_specs=(P(("parts", "dp"), "fsdp"), P(("parts", "dp"), None), P(("parts", "dp"))),
        check_vma=False,
    )
```

```python
import functools

import jax
import jax.numpy as jnp
from jax import lax
from jax.experimental import pallas as pl
from jax.experimental.pallas import tpu as pltpu
from jax.sharding import PartitionSpec as P

HS = 128
SEQ_G = 3


EPSILON = 1e-05


def norm_rows(values):
    average = jnp.mean(values, -1, keepdims=True)
    centred = values - average
    spread = jnp.mean(centred * centred, -1, keepdims=True)
    return centred * lax.rsqrt(spread + EPSILON)


def rotate(field, position):
    half_width = field.shape[-1] // 2
    frequency = 10000.0 ** (-2.0 * jnp.arange(half_width, dtype=jnp.float32) / field.shape[-1])
    angles = position.astype(jnp.float32)[:, None] * frequency[None, :]
    angles = jnp.concatenate([angles, angles], -1)[:, None, :]
    turned = jnp.concatenate([-field[..., half_width:], field[..., :half_width]], -1)
    return field * jnp.cos(angles) + turned * jnp.sin(angles)


def layout(lengths, count):
    ends = jnp.cumsum(lengths)
    starts = ends - lengths
    tok_index = jnp.arange(count, dtype=jnp.int32)
    inside = (tok_index[:, None] >= starts[None, :]) & (tok_index[:, None] < ends[None, :])
    labels = jnp.arange(lengths.shape[0], dtype=jnp.int32)
    segment = jnp.sum(jnp.where(inside, labels[None, :], 0), 1)
    position = tok_index - jnp.sum(jnp.where(inside, starts[None, :], 0), 1)
    return (segment, position, starts)


def attend(queries, key_rows, value_rows, same_seq):

    def one_head(triple):
        query_head, key_head, value_head = triple
        scores = jnp.dot(query_head, key_head.T, preferred_element_type=jnp.float32)
        scores = jnp.where(same_seq, scores, -1e30)
        weights = jax.nn.softmax(scores, -1).astype(jnp.bfloat16)
        return jnp.dot(weights, value_head, preferred_element_type=jnp.float32).astype(jnp.bfloat16)

    stacked = lax.map(
        one_head,
        (queries.transpose(1, 0, 2), key_rows.transpose(1, 0, 2), value_rows.transpose(1, 0, 2)),
    )
    return stacked.transpose(1, 0, 2).reshape(queries.shape[0], -1)


def target_score(logits, target_ids):
    vocab_index = jnp.arange(logits.shape[1], dtype=jnp.int32)
    target = jnp.sum(jnp.where(vocab_index[None, :] == target_ids[:, None], logits, 0.0), 1)
    return target - jax.nn.logsumexp(logits, -1)


def per_device_any(
    hidden, lengths, mask_pos, token_ids, assignment, w_query, w_key, w_value, w_out, embed
):
    tokens_here = hidden.shape[0]
    gathered = lax.all_gather(hidden, "fsdp", axis=1, tiled=True)
    normed = norm_rows(gathered.astype(jnp.float32)).astype(jnp.bfloat16)
    query_sum = jnp.dot(
        normed,
        lax.all_gather(w_query, "dp", axis=0, tiled=True),
        preferred_element_type=jnp.float32,
    )
    key_sum = jnp.dot(
        normed, lax.all_gather(w_key, "dp", axis=0, tiled=True), preferred_element_type=jnp.float32
    )
    value_sum = jnp.dot(
        normed,
        lax.all_gather(w_value, "dp", axis=0, tiled=True),
        preferred_element_type=jnp.float32,
    )
    heads_here = w_query.shape[1] // HS
    segment, position, starts = layout(lengths, tokens_here)
    queries = rotate(
        (query_sum * HS ** (-0.5)).reshape(tokens_here, heads_here, HS), position
    ).astype(jnp.bfloat16)
    key_rows = rotate(key_sum.reshape(tokens_here, heads_here, HS), position).astype(jnp.bfloat16)
    value_rows = value_sum.astype(jnp.bfloat16).reshape(tokens_here, heads_here, HS)
    context = attend(queries, key_rows, value_rows, segment[:, None] == segment[None, :])
    partials = jnp.dot(
        context, lax.all_gather(w_out, "dp", axis=1, tiled=True), preferred_element_type=jnp.float32
    )
    attended = lax.psum_scatter(
        partials.astype(jnp.bfloat16), "fsdp", scatter_dimension=1, tiled=True
    ).astype(jnp.float32)
    states = (hidden.astype(jnp.float32) + attended).astype(jnp.bfloat16)
    picked = starts + mask_pos
    chosen = jnp.arange(tokens_here, dtype=jnp.int32)[None, :] == picked[:, None]
    local_rows = jnp.dot(
        chosen.astype(jnp.bfloat16), states, preferred_element_type=jnp.float32
    ).astype(jnp.bfloat16)
    local_ids = jnp.sum(jnp.where(chosen, token_ids[None, :], 0), 1)
    row_full = lax.all_gather(local_rows, "fsdp", axis=1, tiled=True)
    owned_slots = lax.axis_index("dp") * SEQ_G + jnp.arange(SEQ_G, dtype=jnp.int32)
    all_rows, all_ids, all_owner = (
        lax.all_gather(row_full, "dp", axis=0, tiled=True),
        lax.all_gather(local_ids, "dp", axis=0, tiled=True),
        lax.all_gather(assignment, "dp", axis=0, tiled=True),
    )
    match_owner = all_owner[None, :] == owned_slots[:, None]
    mine_rows = jnp.dot(
        match_owner.astype(jnp.bfloat16), all_rows, preferred_element_type=jnp.float32
    ).astype(jnp.bfloat16)
    mine_ids = jnp.sum(jnp.where(match_owner, all_ids[None, :], 0), 1).astype(jnp.int32)
    normed_rows = norm_rows(mine_rows.astype(jnp.float32)).astype(jnp.bfloat16)
    logits = jnp.dot(normed_rows, embed.T, preferred_element_type=jnp.float32)
    scored = target_score(logits, mine_ids)
    return (states, logits, scored)

F32 = jnp.float32
BF16 = jnp.bfloat16
VMEM_LIMIT = 60 * 1024 * 1024
SMEM_SPEC = pl.BlockSpec(memory_space=pltpu.SMEM)
HBM_SPEC = pl.BlockSpec(memory_space=pltpu.HBM)


def params(*semantics, limit=VMEM_LIMIT):
    return pltpu.CompilerParams(
        vmem_limit_bytes=limit, dimension_semantics=semantics or None
    )


def norm_kernel(column_ref, picked_ref, x_ref, out_ref, rows_ref):
    blocks, size, width = x_ref.shape
    count = blocks * width
    base = pl.program_id(0) * size
    slot = lax.broadcasted_iota(jnp.int32, (rows_ref.shape[1], size), 0)
    row = lax.broadcasted_iota(jnp.int32, (rows_ref.shape[1], size), 1) + base
    hit = sum(
        ((slot == j) & (row == picked_ref[j])).astype(F32) for j in range(picked_ref.shape[0])
    ).astype(BF16)

    @pl.when(pl.program_id(0) == 0)
    def _():
        rows_ref[...] = jnp.zeros_like(rows_ref)

    for b in range(blocks):
        rows_ref[b ^ column_ref[0]] += jnp.dot(hit, x_ref[b], preferred_element_type=F32)
    values = [x_ref[b].astype(F32) for b in range(blocks)]
    average = sum(jnp.sum(v, -1, keepdims=True) for v in values) / count
    centred = [v - average for v in values]
    spread = sum(jnp.sum(v * v, -1, keepdims=True) for v in centred) / count
    scale = lax.rsqrt(spread + EPSILON)
    for b in range(blocks):
        out_ref[:, b * width : (b + 1) * width] = (centred[b] * scale).astype(BF16)


def norm_blocks(column, picked, stack, row_block=224):
    blocks, rows, width = stack.shape
    return pl.pallas_call(
        norm_kernel,
        grid=(rows // row_block,),
        in_specs=[
            SMEM_SPEC,
            SMEM_SPEC,
            pl.BlockSpec((blocks, row_block, width), lambda i: (0, i, 0)),
        ],
        out_specs=[
            pl.BlockSpec((row_block, blocks * width), lambda i: (i, 0)),
            pl.BlockSpec((blocks, 8, width), lambda i: (0, 0, 0)),
        ],
        out_shape=[
            jax.ShapeDtypeStruct((rows, blocks * width), BF16),
            jax.ShapeDtypeStruct((blocks, 8, width), F32),
        ],
        compiler_params=params("arbitrary"),
        cost_estimate=pl.CostEstimate(
            flops=8 * stack.size, bytes_accessed=4 * stack.size, transcendentals=rows
        ),
        name="norm_rows",
    )(column[None].astype(jnp.int32), picked, stack)


def shard_parts(part, shard, half):
    if len(shard) == 2:
        mine, other = shard
        return [
            (mine, pl.multiple_of(part * half, half)),
            (other, pl.multiple_of((1 - part) * half, half)),
        ]
    return [(shard[0].at[pl.ds(j * half, half)], j * half) for j in range(2)]


def take_shards(refs, lengths):
    return [tuple(refs.pop(0) for _ in range(n)) for n in lengths]


def project_kernel(scale, rotated, lengths, place_ref, x_ref, *refs):
    refs = list(refs)
    shards = take_shards(refs, lengths)
    if rotated:
        cos, sin = refs.pop(0)[...], refs.pop(0)[...]
    out_ref, wbuf, sems = refs
    depth, width = shards[0][0].shape
    half = depth // 2

    @pl.when(pl.program_id(0) == 0)
    def _():
        copies = []
        for k, shard in enumerate(shards):
            for j, (source, row) in enumerate(shard_parts(place_ref[0], shard, half)):
                row = pl.multiple_of(place_ref[1 + k] * depth + row, half)
                copies.append(
                    pltpu.make_async_copy(source, wbuf.at[pl.ds(row, half)], sems.at[k, j])
                )
        for copy in copies:
            copy.start()
        for copy in copies:
            copy.wait()

    total = jnp.dot(x_ref[...], wbuf[...], preferred_element_type=F32)
    if not rotated:
        out_ref[...] = total.astype(BF16)
        return
    if scale is not None:
        total = total * scale
    for h in range(width // HS):
        field = total[:, h * HS : (h + 1) * HS]
        turned = pltpu.roll(field, HS // 2, 1)
        out_ref[:, h * HS : (h + 1) * HS] = (field * cos + turned * sin).astype(BF16)


def project(place, normed, shards, scale=None, turn=(), row_block=448):
    rows, features = normed.shape
    width = shards[0][0].shape[1]
    flat = [ref for shard in shards for ref in shard]
    in_specs = [SMEM_SPEC, pl.BlockSpec((row_block, features), lambda i: (i, 0))]
    in_specs += [HBM_SPEC] * len(flat)
    in_specs += [pl.BlockSpec((row_block, HS), lambda i: (i, 0)) for _ in turn]
    return pl.pallas_call(
        functools.partial(
            project_kernel, scale, bool(turn), [len(shard) for shard in shards]
        ),
        grid=(rows // row_block,),
        in_specs=in_specs,
        out_specs=pl.BlockSpec((row_block, width), lambda i: (i, 0)),
        out_shape=jax.ShapeDtypeStruct((rows, width), BF16),
        scratch_shapes=[
            pltpu.VMEM((features, width), BF16),
            pltpu.SemaphoreType.DMA((4, 2)),
        ],
        compiler_params=params("arbitrary"),
        cost_estimate=pl.CostEstimate(
            flops=2 * rows * features * width,
            bytes_accessed=2 * (normed.size + (features + rows) * width),
            transcendentals=0,
        ),
        name="project",
    )(place, normed, *flat, *turn)


def attend_kernel(place_ref, ends_ref, q_ref, k_ref, v_ref, out_ref, *, row_block):
    count = k_ref.shape[0]
    base = place_ref[1] * q_ref.shape[0]
    col = lax.broadcasted_iota(jnp.int32, (1, count), 1)
    sequences = ends_ref.shape[0]
    col_label = sum((col >= ends_ref[j]).astype(jnp.int32) for j in range(sequences - 1))
    for r in range(q_ref.shape[0] // row_block):
        span = slice(r * row_block, (r + 1) * row_block)
        row = lax.broadcasted_iota(jnp.int32, (row_block, 1), 0) + (base + r * row_block)
        row_label = sum((row >= ends_ref[j]).astype(jnp.int32) for j in range(sequences - 1))
        for h in range(q_ref.shape[1] // HS):
            head = slice(h * HS, (h + 1) * HS)
            scores = lax.dot_general(
                q_ref[span, head],
                k_ref[:, head],
                (((1,), (1,)), ((), ())),
                preferred_element_type=F32,
            )
            scores = jnp.where(row_label == col_label, scores, -1e30)
            top = jnp.max(scores, -1, keepdims=True)
            raised = jnp.exp(scores - top)
            weights = raised * (1.0 / jnp.sum(raised, -1, keepdims=True))
            out_ref[span, head] = jnp.dot(
                weights.astype(BF16), v_ref[:, head], preferred_element_type=F32
            ).astype(BF16)


def attention(place, ends, queries, key_rows, value_rows, row_block=448, group=5):
    rows, columns = queries.shape
    half = rows // 2
    heads = columns // HS
    wide = group * HS
    return pl.pallas_call(
        functools.partial(attend_kernel, row_block=row_block),
        grid_spec=pltpu.PrefetchScalarGridSpec(
            num_scalar_prefetch=2,
            grid=(heads // group,),
            in_specs=[
                pl.BlockSpec((half, wide), lambda h, place, ends: (place[1], h)),
                pl.BlockSpec((rows, wide), lambda h, place, ends: (0, h)),
                pl.BlockSpec((rows, wide), lambda h, place, ends: (0, h)),
            ],
            out_specs=pl.BlockSpec((half, wide), lambda h, place, ends: (0, h)),
        ),
        out_shape=jax.ShapeDtypeStruct((half, columns), BF16),
        compiler_params=params("arbitrary"),
        cost_estimate=pl.CostEstimate(
            flops=4 * half * rows * columns,
            bytes_accessed=6 * rows * columns,
            transcendentals=half * rows * heads,
        ),
        name="attention",
    )(place, ends, queries, key_rows, value_rows)


def out_kernel(adding, base, lengths, place_ref, *refs):
    refs = list(refs)
    if adding:
        x_ref, come_ref = refs.pop(0), refs.pop(0)
    else:
        picked_ref, x_ref, kept_ref = refs.pop(0), refs.pop(0), refs.pop(0)
    shards = take_shards(refs, lengths)
    out_ref = refs.pop(0)
    if not adding:
        rows_ref, marked = refs.pop(0), refs.pop()
    wbuf, sems = refs
    block = pl.program_id(0)
    half = wbuf.shape[1] // 2
    part, core = place_ref[0], place_ref[5]

    @pl.when(block == 0)
    def _():
        for k, shard in enumerate(shards):
            spot = place_ref[1 + k] - base

            @pl.when((spot >= 0) & (spot < 2))
            def _():
                for j, (source, row) in enumerate(shard_parts(part, shard, half)):
                    pltpu.make_async_copy(
                        source, wbuf.at[spot, pl.ds(row, half)], sems.at[spot, j]
                    ).start()

        if not adding:
            size = x_ref.shape[0]
            slot = lax.broadcasted_iota(jnp.int32, (marked.shape[0], size), 0)
            row = lax.broadcasted_iota(jnp.int32, (marked.shape[0], size), 1)
            total = None
            for ref, first in ((x_ref, (1 - core) * size), (kept_ref, core * size)):
                hit = sum(
                    ((slot == j) & (row + first == picked_ref[j])).astype(F32)
                    for j in range(picked_ref.shape[0])
                )
                term = jnp.dot(hit.astype(BF16), ref[...], preferred_element_type=F32)
                total = term if total is None else total + term
            marked[...] = total.astype(BF16)

    for j in range(2):
        pltpu.make_async_copy(
            shards[0][0].at[pl.ds(0, half)],
            wbuf.at[block, pl.ds(j * half, half)],
            sems.at[block, j],
        ).wait()
    total = jnp.dot(x_ref[...], wbuf[block], preferred_element_type=F32)
    if adding:
        total = total + come_ref[...].astype(F32)
    else:
        rows_ref[...] = jnp.dot(marked[...], wbuf[block], preferred_element_type=F32)
    out_ref[...] = total.astype(BF16)


def out_project(place, context, shards, base, come=None, picked=None, kept=None):
    half, depth = context.shape
    width = shards[0][0].shape[1]
    flat = [ref for shard in shards for ref in shard]
    adding = come is not None
    whole = pl.BlockSpec((half, depth), lambda j: (0, 0))
    if adding:
        operands = [place, context, come]
        in_specs = [SMEM_SPEC, whole]
        in_specs += [pl.BlockSpec((None, half, width), lambda j: (1 - j, 0, 0))]
    else:
        operands = [place, picked, context, kept]
        in_specs = [SMEM_SPEC, SMEM_SPEC, whole, whole]
    out_specs = [pl.BlockSpec((None, half, width), lambda j: (j, 0, 0))]
    out_shape = [jax.ShapeDtypeStruct((2, half, width), BF16)]
    scratch = [pltpu.VMEM((2, depth, width), BF16), pltpu.SemaphoreType.DMA((2, 2))]
    if not adding:
        out_specs.append(pl.BlockSpec((None, 8, width), lambda j: (j, 0, 0)))
        out_shape.append(jax.ShapeDtypeStruct((2, 8, width), F32))
        scratch.append(pltpu.VMEM((8, depth), BF16))
    return pl.pallas_call(
        functools.partial(out_kernel, adding, base, [len(shard) for shard in shards]),
        grid=(2,),
        in_specs=in_specs + [HBM_SPEC] * len(flat),
        out_specs=out_specs,
        out_shape=out_shape,
        scratch_shapes=scratch,
        compiler_params=params("arbitrary", limit=VMEM_LIMIT),
        cost_estimate=pl.CostEstimate(
            flops=4 * half * depth * width,
            bytes_accessed=2 * (half * depth + 2 * (depth + (1 + adding) * half) * width),
            transcendentals=0,
        ),
        name="out_project",
    )(*operands, *flat)


def tie(value, *earlier):
    return lax.optimization_barrier((value, *earlier))[0]


class WeightRing:
    def __init__(self, dp):
        self.dp = dp
        self.part = lax.axis_index("parts")
        self.along, self.across, self.shards = [], [], []

    def ring(self, value, step):
        return lax.ppermute(value, "dp", [(i, (i + step) % self.dp) for i in range(self.dp)])

    def step(self, value, step, before=(), before_swap=(), gather=False):
        i = len(self.along)
        waits = list(before) + self.along[i - 2 : i - 1] if i >= 2 else list(before)
        self.along.append(self.ring(tie(value, *waits), step))
        if gather:
            whole = lax.all_gather(self.along[i], "parts", axis=0, tiled=True)
            self.shards.append((whole,))
            return
        waits = self.across[-2:-1]
        self.across.append(
            lax.ppermute(tie(self.along[i], *waits, *before_swap), "parts", [(0, 1), (1, 0)])
        )
        self.shards.append((self.along[i], self.across[-1]))

    def half(self, weight):
        size = weight.shape[0] // 2
        return lax.dynamic_slice_in_dim(weight, self.part * size, size, 0)

    def pieces(self, group):
        first = 3 * group
        return [self.shards[i] for i in (first, first + 2, first + 1)]


def per_device(
    hidden, lengths, mask_pos, token_ids, assignment, w_query, w_key, w_value, w_out, embed
):
    dp, fsdp = 4, 4
    rows, width = hidden.shape
    half = rows // 2
    sequences = lengths.shape[0]
    part = lax.axis_index("parts")
    group = lax.axis_index("dp")
    column = lax.axis_index("fsdp")
    core = column % 2
    ring_order = [lax.rem(group + dp - k, dp) for k in range(dp)]
    place = jnp.stack([part] + ring_order).astype(jnp.int32)
    stack = lax.all_gather(hidden, "fsdp", axis=0, tiled=False)
    segment, position, starts = layout(lengths, rows)
    half_width = HS // 2
    frequency = 10000.0 ** (-2.0 * jnp.arange(half_width, dtype=F32) / HS)
    angles = position.astype(F32)[:, None] * frequency[None, :]
    sine, cosine = jnp.sin(angles), jnp.cos(angles)
    turn = (jnp.concatenate([cosine, cosine], -1), jnp.concatenate([-sine, sine], -1))
    picked = starts + mask_pos
    chosen = jnp.arange(rows, dtype=jnp.int32)[None, :] == picked[:, None]
    local_ids = jnp.sum(jnp.where(chosen, token_ids[None, :], 0), 1)

    ends = jnp.cumsum(lengths)
    keep_place = jnp.stack([part, core]).astype(jnp.int32)
    send_place = jnp.stack([part, 1 - core]).astype(jnp.int32)
    out_place = jnp.stack([part] + [s ^ column for s in ring_order] + [core]).astype(jnp.int32)

    def swap_by(value, mask):
        return lax.ppermute(value, "fsdp", [(i, i ^ mask) for i in range(fsdp)])

    def by_offset(blocks):
        return jnp.stack(
            [
                lax.dynamic_index_in_dim(blocks, column ^ r, 0, keepdims=False)
                for r in range(fsdp)
            ]
        )

    extra = jnp.stack([local_ids, assignment], 1).astype(BF16)
    extra = jnp.pad(extra, ((0, 8 - sequences), (0, width - 2)))[None]

    ring = WeightRing(dp)
    mine = ring.half(w_key)
    ring.step(mine, 1)
    ring.step(mine, -1)
    ring.step(ring.along[0], 1)
    mine = ring.half(w_query)
    ring.step(mine, 1)
    ring.step(mine, -1)
    normed, hidden_rows = norm_blocks(column, picked, stack)
    ring.step(ring.along[3], 1)
    key_rows = project(place, normed, [(w_key,), *ring.pieces(0)], None, turn)
    mine = ring.half(w_value)
    ring.step(mine, 1, before=[normed])
    ring.step(mine, -1, before=[key_rows])
    ring.step(ring.along[6], 1)
    queries = project(place, normed, [(w_query,), *ring.pieces(1)], HS ** (-0.5), turn)
    mine = ring.half(w_out)
    ring.step(mine, 1)
    value_rows = project(place, normed, [(w_value,), *ring.pieces(2)])
    ring.step(mine, -1, before=[queries], before_swap=[value_rows])
    context_sent = attention(send_place, ends, queries, key_rows, value_rows)
    last_along = ring.ring(tie(ring.along[9], ring.along[9]), 1)
    last_other = ring.ring(tie(ring.across[-2], ring.along[10], context_sent), 1)
    out_in = [(w_out,), ring.shards[9], (last_along, last_other), ring.shards[10]]
    context_kept = attention(keep_place, ends, queries, key_rows, tie(value_rows, context_sent))

    def send(base, *before):
        return out_project(
            out_place, tie(context_sent, *before), out_in, base, None, picked, context_kept
        )

    sent_far, rows_far = send(2)
    arrived_far = swap_by(sent_far, 1)
    sent_near, rows_near = send(0, sent_far)
    arrived_near = swap_by(sent_near, 1)
    (chip_far,) = out_project(
        out_place, tie(context_kept, sent_near), out_in, 2, arrived_far
    )
    crossed = swap_by(chip_far, 2)
    (chip_near,) = out_project(
        out_place, tie(context_kept, chip_far), out_in, 0, arrived_near
    )

    own_sum = jnp.concatenate([rows_near, rows_far], 0)
    row_sum = own_sum
    for mask in range(1, fsdp):
        come = swap_by(own_sum, mask)
        row_sum = row_sum + jnp.stack([come[r ^ mask] for r in range(fsdp)])
    full_rows = (hidden_rows + row_sum).astype(BF16)
    packet = jnp.concatenate([full_rows, extra], 0)
    packets = [packet] + [ring.ring(packet, shift) for shift in range(1, dp)]
    packets = tie(jnp.stack(packets), crossed)[:, :, :sequences]
    all_rows = by_offset(packets[:, :dp].transpose(1, 0, 2, 3).reshape(dp, dp * sequences, width))
    all_rows = all_rows.transpose(1, 0, 2).reshape(dp * sequences, dp * width)
    all_ids = packets[:, dp, :, 0].reshape(-1).astype(jnp.int32)
    all_owner = packets[:, dp, :, 1].reshape(-1).astype(jnp.int32)
    owned = group * sequences + jnp.arange(sequences, dtype=jnp.int32)
    match = all_owner[None, :] == owned[:, None]
    mine_rows = jnp.dot(match.astype(BF16), all_rows, preferred_element_type=F32)
    mine_ids = jnp.sum(jnp.where(match, all_ids[None, :], 0), 1).astype(jnp.int32)
    normed_rows = norm_rows(mine_rows).astype(BF16)
    logits = jnp.dot(normed_rows, embed.T, preferred_element_type=F32)
    scored = target_score(logits, mine_ids)

    def block_rows(index, place_in_chip):
        before = lax.dynamic_slice(stack, (index, core * half, 0), (1, half, width))[0]
        summed = chip_near[place_in_chip].astype(F32) + crossed[place_in_chip].astype(F32)
        return (before.astype(F32) + summed).astype(BF16)

    other_rows = swap_by(block_rows(column ^ 1, 1), 1)
    own_rows = block_rows(column, 0)
    states = jnp.where(
        core == 0,
        jnp.concatenate([own_rows, other_rows], 0),
        jnp.concatenate([other_rows, own_rows], 0),
    )
    return (states, logits, scored)


def ring_fits(mesh):
    return (mesh.shape["parts"], mesh.shape["dp"], mesh.shape["fsdp"]) == (2, 4, 4)


def solution(mesh):
    return jax.shard_map(
        per_device if ring_fits(mesh) else per_device_any,
        mesh=mesh,
        in_specs=(
            P(("parts", "dp"), "fsdp"),
            P(("parts", "dp")),
            P(("parts", "dp")),
            P(("parts", "dp")),
            P(("parts", "dp")),
            P("dp", "fsdp"),
            P("dp", "fsdp"),
            P("dp", "fsdp"),
            P("fsdp", "dp"),
            P(),
        ),
        out_specs=(P(("parts", "dp"), "fsdp"), P(("parts", "dp"), None), P(("parts", "dp"))),
        check_vma=False,
    )
```

```python
import functools

import jax
import jax.numpy as jnp
from jax import lax
from jax.experimental import pallas as pl
from jax.experimental.pallas import tpu as pltpu
from jax.sharding import PartitionSpec as P

HS = 128
SEQ_G = 3


EPSILON = 1e-05


def norm_rows(values):
    average = jnp.mean(values, -1, keepdims=True)
    centred = values - average
    spread = jnp.mean(centred * centred, -1, keepdims=True)
    return centred * lax.rsqrt(spread + EPSILON)


def rotate(field, position):
    half_width = field.shape[-1] // 2
    frequency = 10000.0 ** (-2.0 * jnp.arange(half_width, dtype=jnp.float32) / field.shape[-1])
    angles = position.astype(jnp.float32)[:, None] * frequency[None, :]
    angles = jnp.concatenate([angles, angles], -1)[:, None, :]
    turned = jnp.concatenate([-field[..., half_width:], field[..., :half_width]], -1)
    return field * jnp.cos(angles) + turned * jnp.sin(angles)


def layout(lengths, count):
    ends = jnp.cumsum(lengths)
    starts = ends - lengths
    tok_index = jnp.arange(count, dtype=jnp.int32)
    inside = (tok_index[:, None] >= starts[None, :]) & (tok_index[:, None] < ends[None, :])
    labels = jnp.arange(lengths.shape[0], dtype=jnp.int32)
    segment = jnp.sum(jnp.where(inside, labels[None, :], 0), 1)
    position = tok_index - jnp.sum(jnp.where(inside, starts[None, :], 0), 1)
    return (segment, position, starts)


def attend(queries, key_rows, value_rows, same_seq):

    def one_head(triple):
        query_head, key_head, value_head = triple
        scores = jnp.dot(query_head, key_head.T, preferred_element_type=jnp.float32)
        scores = jnp.where(same_seq, scores, -1e30)
        weights = jax.nn.softmax(scores, -1).astype(jnp.bfloat16)
        return jnp.dot(weights, value_head, preferred_element_type=jnp.float32).astype(jnp.bfloat16)

    stacked = lax.map(
        one_head,
        (queries.transpose(1, 0, 2), key_rows.transpose(1, 0, 2), value_rows.transpose(1, 0, 2)),
    )
    return stacked.transpose(1, 0, 2).reshape(queries.shape[0], -1)


def target_score(logits, target_ids):
    vocab_index = jnp.arange(logits.shape[1], dtype=jnp.int32)
    target = jnp.sum(jnp.where(vocab_index[None, :] == target_ids[:, None], logits, 0.0), 1)
    return target - jax.nn.logsumexp(logits, -1)


def per_device_any(
    hidden, lengths, mask_pos, token_ids, assignment, w_query, w_key, w_value, w_out, embed
):
    tokens_here = hidden.shape[0]
    gathered = lax.all_gather(hidden, "fsdp", axis=1, tiled=True)
    normed = norm_rows(gathered.astype(jnp.float32)).astype(jnp.bfloat16)
    query_sum = jnp.dot(
        normed,
        lax.all_gather(w_query, "dp", axis=0, tiled=True),
        preferred_element_type=jnp.float32,
    )
    key_sum = jnp.dot(
        normed, lax.all_gather(w_key, "dp", axis=0, tiled=True), preferred_element_type=jnp.float32
    )
    value_sum = jnp.dot(
        normed,
        lax.all_gather(w_value, "dp", axis=0, tiled=True),
        preferred_element_type=jnp.float32,
    )
    heads_here = w_query.shape[1] // HS
    segment, position, starts = layout(lengths, tokens_here)
    queries = rotate(
        (query_sum * HS ** (-0.5)).reshape(tokens_here, heads_here, HS), position
    ).astype(jnp.bfloat16)
    key_rows = rotate(key_sum.reshape(tokens_here, heads_here, HS), position).astype(jnp.bfloat16)
    value_rows = value_sum.astype(jnp.bfloat16).reshape(tokens_here, heads_here, HS)
    context = attend(queries, key_rows, value_rows, segment[:, None] == segment[None, :])
    partials = jnp.dot(
        context, lax.all_gather(w_out, "dp", axis=1, tiled=True), preferred_element_type=jnp.float32
    )
    attended = lax.psum_scatter(
        partials.astype(jnp.bfloat16), "fsdp", scatter_dimension=1, tiled=True
    ).astype(jnp.float32)
    states = (hidden.astype(jnp.float32) + attended).astype(jnp.bfloat16)
    picked = starts + mask_pos
    chosen = jnp.arange(tokens_here, dtype=jnp.int32)[None, :] == picked[:, None]
    local_rows = jnp.dot(
        chosen.astype(jnp.bfloat16), states, preferred_element_type=jnp.float32
    ).astype(jnp.bfloat16)
    local_ids = jnp.sum(jnp.where(chosen, token_ids[None, :], 0), 1)
    row_full = lax.all_gather(local_rows, "fsdp", axis=1, tiled=True)
    owned_slots = lax.axis_index("dp") * SEQ_G + jnp.arange(SEQ_G, dtype=jnp.int32)
    all_rows, all_ids, all_owner = (
        lax.all_gather(row_full, "dp", axis=0, tiled=True),
        lax.all_gather(local_ids, "dp", axis=0, tiled=True),
        lax.all_gather(assignment, "dp", axis=0, tiled=True),
    )
    match_owner = all_owner[None, :] == owned_slots[:, None]
    mine_rows = jnp.dot(
        match_owner.astype(jnp.bfloat16), all_rows, preferred_element_type=jnp.float32
    ).astype(jnp.bfloat16)
    mine_ids = jnp.sum(jnp.where(match_owner, all_ids[None, :], 0), 1).astype(jnp.int32)
    normed_rows = norm_rows(mine_rows.astype(jnp.float32)).astype(jnp.bfloat16)
    logits = jnp.dot(normed_rows, embed.T, preferred_element_type=jnp.float32)
    scored = target_score(logits, mine_ids)
    return (states, logits, scored)

F32 = jnp.float32
BF16 = jnp.bfloat16
VMEM_LIMIT = 60 * 1024 * 1024
SMEM_SPEC = pl.BlockSpec(memory_space=pltpu.SMEM)
HBM_SPEC = pl.BlockSpec(memory_space=pltpu.HBM)


def params(*semantics, limit=VMEM_LIMIT):
    return pltpu.CompilerParams(
        vmem_limit_bytes=limit, dimension_semantics=semantics or None
    )


def norm_kernel(column_ref, picked_ref, x_ref, out_ref, rows_ref):
    blocks, size, width = x_ref.shape
    count = blocks * width
    base = pl.program_id(0) * size
    slot = lax.broadcasted_iota(jnp.int32, (rows_ref.shape[1], size), 0)
    row = lax.broadcasted_iota(jnp.int32, (rows_ref.shape[1], size), 1) + base
    hit = sum(
        ((slot == j) & (row == picked_ref[j])).astype(F32) for j in range(picked_ref.shape[0])
    ).astype(BF16)

    @pl.when(pl.program_id(0) == 0)
    def _():
        rows_ref[...] = jnp.zeros_like(rows_ref)

    for b in range(blocks):
        rows_ref[b ^ column_ref[0]] += jnp.dot(hit, x_ref[b], preferred_element_type=F32)
    values = [x_ref[b].astype(F32) for b in range(blocks)]
    average = sum(jnp.sum(v, -1, keepdims=True) for v in values) / count
    centred = [v - average for v in values]
    spread = sum(jnp.sum(v * v, -1, keepdims=True) for v in centred) / count
    scale = lax.rsqrt(spread + EPSILON)
    for b in range(blocks):
        out_ref[:, b * width : (b + 1) * width] = (centred[b] * scale).astype(BF16)


def norm_blocks(column, picked, stack, row_block=224):
    blocks, rows, width = stack.shape
    return pl.pallas_call(
        norm_kernel,
        grid=(rows // row_block,),
        in_specs=[
            SMEM_SPEC,
            SMEM_SPEC,
            pl.BlockSpec((blocks, row_block, width), lambda i: (0, i, 0)),
        ],
        out_specs=[
            pl.BlockSpec((row_block, blocks * width), lambda i: (i, 0)),
            pl.BlockSpec((blocks, 8, width), lambda i: (0, 0, 0)),
        ],
        out_shape=[
            jax.ShapeDtypeStruct((rows, blocks * width), BF16),
            jax.ShapeDtypeStruct((blocks, 8, width), F32),
        ],
        compiler_params=params("arbitrary"),
        cost_estimate=pl.CostEstimate(
            flops=8 * stack.size, bytes_accessed=4 * stack.size, transcendentals=rows
        ),
        name="norm_rows",
    )(column[None].astype(jnp.int32), picked, stack)


def shard_parts(part, shard, half):
    if len(shard) == 2:
        mine, other = shard
        return [
            (mine, pl.multiple_of(part * half, half)),
            (other, pl.multiple_of((1 - part) * half, half)),
        ]
    return [(shard[0].at[pl.ds(j * half, half)], j * half) for j in range(2)]


def take_shards(refs, lengths):
    return [tuple(refs.pop(0) for _ in range(n)) for n in lengths]


def project_kernel(scale, rotated, lengths, place_ref, x_ref, *refs):
    refs = list(refs)
    shards = take_shards(refs, lengths)
    if rotated:
        cos, sin = refs.pop(0)[...], refs.pop(0)[...]
    out_ref, wbuf, sems = refs
    depth, width = shards[0][0].shape
    half = depth // 2

    @pl.when(pl.program_id(0) == 0)
    def _():
        copies = []
        for k, shard in enumerate(shards):
            for j, (source, row) in enumerate(shard_parts(place_ref[0], shard, half)):
                row = pl.multiple_of(place_ref[1 + k] * depth + row, half)
                copies.append(
                    pltpu.make_async_copy(source, wbuf.at[pl.ds(row, half)], sems.at[k, j])
                )
        for copy in copies:
            copy.start()
        for copy in copies:
            copy.wait()

    total = jnp.dot(x_ref[...], wbuf[...], preferred_element_type=F32)
    if not rotated:
        out_ref[...] = total.astype(BF16)
        return
    if scale is not None:
        total = total * scale
    for h in range(width // HS):
        field = total[:, h * HS : (h + 1) * HS]
        turned = pltpu.roll(field, HS // 2, 1)
        out_ref[:, h * HS : (h + 1) * HS] = (field * cos + turned * sin).astype(BF16)


def project(place, normed, shards, scale=None, turn=(), row_block=448):
    rows, features = normed.shape
    width = shards[0][0].shape[1]
    flat = [ref for shard in shards for ref in shard]
    in_specs = [SMEM_SPEC, pl.BlockSpec((row_block, features), lambda i: (i, 0))]
    in_specs += [HBM_SPEC] * len(flat)
    in_specs += [pl.BlockSpec((row_block, HS), lambda i: (i, 0)) for _ in turn]
    return pl.pallas_call(
        functools.partial(
            project_kernel, scale, bool(turn), [len(shard) for shard in shards]
        ),
        grid=(rows // row_block,),
        in_specs=in_specs,
        out_specs=pl.BlockSpec((row_block, width), lambda i: (i, 0)),
        out_shape=jax.ShapeDtypeStruct((rows, width), BF16),
        scratch_shapes=[
            pltpu.VMEM((features, width), BF16),
            pltpu.SemaphoreType.DMA((4, 2)),
        ],
        compiler_params=params("arbitrary"),
        cost_estimate=pl.CostEstimate(
            flops=2 * rows * features * width,
            bytes_accessed=2 * (normed.size + (features + rows) * width),
            transcendentals=0,
        ),
        name="project",
    )(place, normed, *flat, *turn)


def attend_kernel(place_ref, ends_ref, q_ref, k_ref, v_ref, out_ref, *, row_block):
    count = k_ref.shape[0]
    base = place_ref[1] * q_ref.shape[0]
    col = lax.broadcasted_iota(jnp.int32, (1, count), 1)
    sequences = ends_ref.shape[0]
    col_label = sum((col >= ends_ref[j]).astype(jnp.int32) for j in range(sequences - 1))
    for r in range(q_ref.shape[0] // row_block):
        span = slice(r * row_block, (r + 1) * row_block)
        row = lax.broadcasted_iota(jnp.int32, (row_block, 1), 0) + (base + r * row_block)
        row_label = sum((row >= ends_ref[j]).astype(jnp.int32) for j in range(sequences - 1))
        for h in range(q_ref.shape[1] // HS):
            head = slice(h * HS, (h + 1) * HS)
            scores = lax.dot_general(
                q_ref[span, head],
                k_ref[:, head],
                (((1,), (1,)), ((), ())),
                preferred_element_type=F32,
            )
            scores = jnp.where(row_label == col_label, scores, -1e30)
            top = jnp.max(scores, -1, keepdims=True)
            raised = jnp.exp(scores - top)
            weights = raised * (1.0 / jnp.sum(raised, -1, keepdims=True))
            out_ref[span, head] = jnp.dot(
                weights.astype(BF16), v_ref[:, head], preferred_element_type=F32
            ).astype(BF16)


def attention(place, ends, queries, key_rows, value_rows, row_block=448, group=5):
    rows, columns = queries.shape
    half = rows // 2
    heads = columns // HS
    wide = group * HS
    return pl.pallas_call(
        functools.partial(attend_kernel, row_block=row_block),
        grid_spec=pltpu.PrefetchScalarGridSpec(
            num_scalar_prefetch=2,
            grid=(heads // group,),
            in_specs=[
                pl.BlockSpec((half, wide), lambda h, place, ends: (place[1], h)),
                pl.BlockSpec((rows, wide), lambda h, place, ends: (0, h)),
                pl.BlockSpec((rows, wide), lambda h, place, ends: (0, h)),
            ],
            out_specs=pl.BlockSpec((half, wide), lambda h, place, ends: (0, h)),
        ),
        out_shape=jax.ShapeDtypeStruct((half, columns), BF16),
        compiler_params=params("arbitrary"),
        cost_estimate=pl.CostEstimate(
            flops=4 * half * rows * columns,
            bytes_accessed=6 * rows * columns,
            transcendentals=half * rows * heads,
        ),
        name="attention",
    )(place, ends, queries, key_rows, value_rows)


def out_kernel(adding, base, lengths, place_ref, *refs):
    refs = list(refs)
    if adding:
        x_ref, come_ref = refs.pop(0), refs.pop(0)
    else:
        picked_ref, x_ref, kept_ref = refs.pop(0), refs.pop(0), refs.pop(0)
    shards = take_shards(refs, lengths)
    out_ref = refs.pop(0)
    if not adding:
        rows_ref, marked = refs.pop(0), refs.pop()
    wbuf, sems = refs
    block = pl.program_id(0)
    half = wbuf.shape[1] // 2
    part, core = place_ref[0], place_ref[5]

    @pl.when(block == 0)
    def _():
        for k, shard in enumerate(shards):
            spot = place_ref[1 + k] - base

            @pl.when((spot >= 0) & (spot < 2))
            def _():
                for j, (source, row) in enumerate(shard_parts(part, shard, half)):
                    pltpu.make_async_copy(
                        source, wbuf.at[spot, pl.ds(row, half)], sems.at[spot, j]
                    ).start()

        if not adding:
            size = x_ref.shape[0]
            slot = lax.broadcasted_iota(jnp.int32, (marked.shape[0], size), 0)
            row = lax.broadcasted_iota(jnp.int32, (marked.shape[0], size), 1)
            total = None
            for ref, first in ((x_ref, (1 - core) * size), (kept_ref, core * size)):
                hit = sum(
                    ((slot == j) & (row + first == picked_ref[j])).astype(F32)
                    for j in range(picked_ref.shape[0])
                )
                term = jnp.dot(hit.astype(BF16), ref[...], preferred_element_type=F32)
                total = term if total is None else total + term
            marked[...] = total.astype(BF16)

    for j in range(2):
        pltpu.make_async_copy(
            shards[0][0].at[pl.ds(0, half)],
            wbuf.at[block, pl.ds(j * half, half)],
            sems.at[block, j],
        ).wait()
    total = jnp.dot(x_ref[...], wbuf[block], preferred_element_type=F32)
    if adding:
        total = total + come_ref[...].astype(F32)
    else:
        rows_ref[...] = jnp.dot(marked[...], wbuf[block], preferred_element_type=F32)
    out_ref[...] = total.astype(BF16)


def out_project(place, context, shards, base, come=None, picked=None, kept=None):
    half, depth = context.shape
    width = shards[0][0].shape[1]
    flat = [ref for shard in shards for ref in shard]
    adding = come is not None
    whole = pl.BlockSpec((half, depth), lambda j: (0, 0))
    if adding:
        operands = [place, context, come]
        in_specs = [SMEM_SPEC, whole]
        in_specs += [pl.BlockSpec((None, half, width), lambda j: (1 - j, 0, 0))]
    else:
        operands = [place, picked, context, kept]
        in_specs = [SMEM_SPEC, SMEM_SPEC, whole, whole]
    out_specs = [pl.BlockSpec((None, half, width), lambda j: (j, 0, 0))]
    out_shape = [jax.ShapeDtypeStruct((2, half, width), BF16)]
    scratch = [pltpu.VMEM((2, depth, width), BF16), pltpu.SemaphoreType.DMA((2, 2))]
    if not adding:
        out_specs.append(pl.BlockSpec((None, 8, width), lambda j: (j, 0, 0)))
        out_shape.append(jax.ShapeDtypeStruct((2, 8, width), F32))
        scratch.append(pltpu.VMEM((8, depth), BF16))
    return pl.pallas_call(
        functools.partial(out_kernel, adding, base, [len(shard) for shard in shards]),
        grid=(2,),
        in_specs=in_specs + [HBM_SPEC] * len(flat),
        out_specs=out_specs,
        out_shape=out_shape,
        scratch_shapes=scratch,
        compiler_params=params("arbitrary", limit=VMEM_LIMIT),
        cost_estimate=pl.CostEstimate(
            flops=4 * half * depth * width,
            bytes_accessed=2 * (half * depth + 2 * (depth + (1 + adding) * half) * width),
            transcendentals=0,
        ),
        name="out_project",
    )(*operands, *flat)


def tie(value, *earlier):
    return lax.optimization_barrier((value, *earlier))[0]


class WeightRing:
    def __init__(self, dp):
        self.dp = dp
        self.part = lax.axis_index("parts")
        self.along, self.across, self.shards = [], [], []

    def ring(self, value, step):
        return lax.ppermute(value, "dp", [(i, (i + step) % self.dp) for i in range(self.dp)])

    def step(self, value, step, before=(), before_swap=(), gather=False):
        i = len(self.along)
        waits = list(before) + self.along[i - 2 : i - 1] if i >= 2 else list(before)
        self.along.append(self.ring(tie(value, *waits), step))
        if gather:
            whole = lax.all_gather(self.along[i], "parts", axis=0, tiled=True)
            self.shards.append((whole,))
            return
        waits = self.across[-2:-1]
        self.across.append(
            lax.ppermute(tie(self.along[i], *waits, *before_swap), "parts", [(0, 1), (1, 0)])
        )
        self.shards.append((self.along[i], self.across[-1]))

    def half(self, weight):
        size = weight.shape[0] // 2
        return lax.dynamic_slice_in_dim(weight, self.part * size, size, 0)

    def pieces(self, group):
        first = 3 * group
        return [self.shards[i] for i in (first, first + 2, first + 1)]


def per_device(
    hidden, lengths, mask_pos, token_ids, assignment, w_query, w_key, w_value, w_out, embed
):
    dp, fsdp = 4, 4
    rows, width = hidden.shape
    half = rows // 2
    sequences = lengths.shape[0]
    part = lax.axis_index("parts")
    group = lax.axis_index("dp")
    column = lax.axis_index("fsdp")
    core = column % 2
    ring_order = [lax.rem(group + dp - k, dp) for k in range(dp)]
    place = jnp.stack([part] + ring_order).astype(jnp.int32)
    stack = lax.all_gather(hidden, "fsdp", axis=0, tiled=False)
    segment, position, starts = layout(lengths, rows)
    half_width = HS // 2
    frequency = 10000.0 ** (-2.0 * jnp.arange(half_width, dtype=F32) / HS)
    angles = position.astype(F32)[:, None] * frequency[None, :]
    sine, cosine = jnp.sin(angles), jnp.cos(angles)
    turn = (jnp.concatenate([cosine, cosine], -1), jnp.concatenate([-sine, sine], -1))
    picked = starts + mask_pos
    chosen = jnp.arange(rows, dtype=jnp.int32)[None, :] == picked[:, None]
    local_ids = jnp.sum(jnp.where(chosen, token_ids[None, :], 0), 1)

    ends = jnp.cumsum(lengths)
    keep_place = jnp.stack([part, core]).astype(jnp.int32)
    send_place = jnp.stack([part, 1 - core]).astype(jnp.int32)
    out_place = jnp.stack([part] + [s ^ column for s in ring_order] + [core]).astype(jnp.int32)

    def swap_by(value, mask):
        return lax.ppermute(value, "fsdp", [(i, i ^ mask) for i in range(fsdp)])

    def by_offset(blocks):
        return jnp.stack(
            [
                lax.dynamic_index_in_dim(blocks, column ^ r, 0, keepdims=False)
                for r in range(fsdp)
            ]
        )

    extra = jnp.stack([local_ids, assignment], 1).astype(BF16)
    extra = jnp.pad(extra, ((0, 8 - sequences), (0, width - 2)))[None]

    ring = WeightRing(dp)
    mine = ring.half(w_key)
    ring.step(mine, 1)
    ring.step(mine, -1)
    ring.step(ring.along[0], 1)
    mine = ring.half(w_query)
    ring.step(mine, 1)
    ring.step(mine, -1)
    normed, hidden_rows = norm_blocks(column, picked, stack)
    ring.step(ring.along[3], 1)
    key_rows = project(place, normed, [(w_key,), *ring.pieces(0)], None, turn)
    mine = ring.half(w_value)
    ring.step(mine, 1, before=[normed])
    queries = project(place, normed, [(w_query,), *ring.pieces(1)], HS ** (-0.5), turn)
    ring.step(mine, -1, before=[key_rows], before_swap=[queries])
    ring.step(ring.along[6], 1)
    mine = ring.half(w_out)
    ring.step(mine, 1)
    value_rows = project(place, normed, [(w_value,), *ring.pieces(2)])
    ring.step(mine, -1, before=[queries], before_swap=[value_rows])
    context_sent = attention(send_place, ends, queries, key_rows, value_rows)
    last_along = ring.ring(tie(ring.along[9], ring.along[9]), 1)
    last_other = ring.ring(tie(ring.across[-2], ring.along[10], context_sent), 1)
    out_in = [(w_out,), ring.shards[9], (last_along, last_other), ring.shards[10]]
    context_kept = attention(keep_place, ends, queries, key_rows, tie(value_rows, context_sent))

    def send(base, *before):
        return out_project(
            out_place, tie(context_sent, *before), out_in, base, None, picked, context_kept
        )

    sent_far, rows_far = send(2)
    arrived_far = swap_by(sent_far, 1)
    sent_near, rows_near = send(0, sent_far)
    arrived_near = swap_by(sent_near, 1)
    (chip_far,) = out_project(
        out_place, tie(context_kept, sent_near), out_in, 2, arrived_far
    )
    crossed = swap_by(chip_far, 2)
    (chip_near,) = out_project(
        out_place, tie(context_kept, chip_far), out_in, 0, arrived_near
    )

    own_sum = jnp.concatenate([rows_near, rows_far], 0)
    row_sum = own_sum
    for mask in range(1, fsdp):
        come = swap_by(own_sum, mask)
        row_sum = row_sum + jnp.stack([come[r ^ mask] for r in range(fsdp)])
    full_rows = (hidden_rows + row_sum).astype(BF16)
    packet = jnp.concatenate([full_rows, extra], 0)
    packets = [packet] + [ring.ring(packet, shift) for shift in range(1, dp)]
    packets = tie(jnp.stack(packets), crossed)[:, :, :sequences]
    all_rows = by_offset(packets[:, :dp].transpose(1, 0, 2, 3).reshape(dp, dp * sequences, width))
    all_rows = all_rows.transpose(1, 0, 2).reshape(dp * sequences, dp * width)
    all_ids = packets[:, dp, :, 0].reshape(-1).astype(jnp.int32)
    all_owner = packets[:, dp, :, 1].reshape(-1).astype(jnp.int32)
    owned = group * sequences + jnp.arange(sequences, dtype=jnp.int32)
    match = all_owner[None, :] == owned[:, None]
    mine_rows = jnp.dot(match.astype(BF16), all_rows, preferred_element_type=F32)
    mine_ids = jnp.sum(jnp.where(match, all_ids[None, :], 0), 1).astype(jnp.int32)
    normed_rows = norm_rows(mine_rows).astype(BF16)
    logits = jnp.dot(normed_rows, embed.T, preferred_element_type=F32)
    scored = target_score(logits, mine_ids)

    def block_rows(index, place_in_chip):
        before = lax.dynamic_slice(stack, (index, core * half, 0), (1, half, width))[0]
        summed = chip_near[place_in_chip].astype(F32) + crossed[place_in_chip].astype(F32)
        return (before.astype(F32) + summed).astype(BF16)

    other_rows = swap_by(block_rows(column ^ 1, 1), 1)
    own_rows = block_rows(column, 0)
    states = jnp.where(
        core == 0,
        jnp.concatenate([own_rows, other_rows], 0),
        jnp.concatenate([other_rows, own_rows], 0),
    )
    return (states, logits, scored)


def ring_fits(mesh):
    return (mesh.shape["parts"], mesh.shape["dp"], mesh.shape["fsdp"]) == (2, 4, 4)


def solution(mesh):
    return jax.shard_map(
        per_device if ring_fits(mesh) else per_device_any,
        mesh=mesh,
        in_specs=(
            P(("parts", "dp"), "fsdp"),
            P(("parts", "dp")),
            P(("parts", "dp")),
            P(("parts", "dp")),
            P(("parts", "dp")),
            P("dp", "fsdp"),
            P("dp", "fsdp"),
            P("dp", "fsdp"),
            P("fsdp", "dp"),
            P(),
        ),
        out_specs=(P(("parts", "dp"), "fsdp"), P(("parts", "dp"), None), P(("parts", "dp"))),
        check_vma=False,
    )
```

```python
import functools

import jax
import jax.numpy as jnp
from jax import lax
from jax.experimental import pallas as pl
from jax.experimental.pallas import tpu as pltpu
from jax.sharding import PartitionSpec as P

HS = 128
SEQ_G = 3


EPSILON = 1e-05


def norm_rows(values):
    average = jnp.mean(values, -1, keepdims=True)
    centred = values - average
    spread = jnp.mean(centred * centred, -1, keepdims=True)
    return centred * lax.rsqrt(spread + EPSILON)


def rotate(field, position):
    half_width = field.shape[-1] // 2
    frequency = 10000.0 ** (-2.0 * jnp.arange(half_width, dtype=jnp.float32) / field.shape[-1])
    angles = position.astype(jnp.float32)[:, None] * frequency[None, :]
    angles = jnp.concatenate([angles, angles], -1)[:, None, :]
    turned = jnp.concatenate([-field[..., half_width:], field[..., :half_width]], -1)
    return field * jnp.cos(angles) + turned * jnp.sin(angles)


def layout(lengths, count):
    ends = jnp.cumsum(lengths)
    starts = ends - lengths
    tok_index = jnp.arange(count, dtype=jnp.int32)
    inside = (tok_index[:, None] >= starts[None, :]) & (tok_index[:, None] < ends[None, :])
    labels = jnp.arange(lengths.shape[0], dtype=jnp.int32)
    segment = jnp.sum(jnp.where(inside, labels[None, :], 0), 1)
    position = tok_index - jnp.sum(jnp.where(inside, starts[None, :], 0), 1)
    return (segment, position, starts)


def attend(queries, key_rows, value_rows, same_seq):

    def one_head(triple):
        query_head, key_head, value_head = triple
        scores = jnp.dot(query_head, key_head.T, preferred_element_type=jnp.float32)
        scores = jnp.where(same_seq, scores, -1e30)
        weights = jax.nn.softmax(scores, -1).astype(jnp.bfloat16)
        return jnp.dot(weights, value_head, preferred_element_type=jnp.float32).astype(jnp.bfloat16)

    stacked = lax.map(
        one_head,
        (queries.transpose(1, 0, 2), key_rows.transpose(1, 0, 2), value_rows.transpose(1, 0, 2)),
    )
    return stacked.transpose(1, 0, 2).reshape(queries.shape[0], -1)


def target_score(logits, target_ids):
    vocab_index = jnp.arange(logits.shape[1], dtype=jnp.int32)
    target = jnp.sum(jnp.where(vocab_index[None, :] == target_ids[:, None], logits, 0.0), 1)
    return target - jax.nn.logsumexp(logits, -1)


def per_device_any(
    hidden, lengths, mask_pos, token_ids, assignment, w_query, w_key, w_value, w_out, embed
):
    tokens_here = hidden.shape[0]
    gathered = lax.all_gather(hidden, "fsdp", axis=1, tiled=True)
    normed = norm_rows(gathered.astype(jnp.float32)).astype(jnp.bfloat16)
    query_sum = jnp.dot(
        normed,
        lax.all_gather(w_query, "dp", axis=0, tiled=True),
        preferred_element_type=jnp.float32,
    )
    key_sum = jnp.dot(
        normed, lax.all_gather(w_key, "dp", axis=0, tiled=True), preferred_element_type=jnp.float32
    )
    value_sum = jnp.dot(
        normed,
        lax.all_gather(w_value, "dp", axis=0, tiled=True),
        preferred_element_type=jnp.float32,
    )
    heads_here = w_query.shape[1] // HS
    segment, position, starts = layout(lengths, tokens_here)
    queries = rotate(
        (query_sum * HS ** (-0.5)).reshape(tokens_here, heads_here, HS), position
    ).astype(jnp.bfloat16)
    key_rows = rotate(key_sum.reshape(tokens_here, heads_here, HS), position).astype(jnp.bfloat16)
    value_rows = value_sum.astype(jnp.bfloat16).reshape(tokens_here, heads_here, HS)
    context = attend(queries, key_rows, value_rows, segment[:, None] == segment[None, :])
    partials = jnp.dot(
        context, lax.all_gather(w_out, "dp", axis=1, tiled=True), preferred_element_type=jnp.float32
    )
    attended = lax.psum_scatter(
        partials.astype(jnp.bfloat16), "fsdp", scatter_dimension=1, tiled=True
    ).astype(jnp.float32)
    states = (hidden.astype(jnp.float32) + attended).astype(jnp.bfloat16)
    picked = starts + mask_pos
    chosen = jnp.arange(tokens_here, dtype=jnp.int32)[None, :] == picked[:, None]
    local_rows = jnp.dot(
        chosen.astype(jnp.bfloat16), states, preferred_element_type=jnp.float32
    ).astype(jnp.bfloat16)
    local_ids = jnp.sum(jnp.where(chosen, token_ids[None, :], 0), 1)
    row_full = lax.all_gather(local_rows, "fsdp", axis=1, tiled=True)
    owned_slots = lax.axis_index("dp") * SEQ_G + jnp.arange(SEQ_G, dtype=jnp.int32)
    all_rows, all_ids, all_owner = (
        lax.all_gather(row_full, "dp", axis=0, tiled=True),
        lax.all_gather(local_ids, "dp", axis=0, tiled=True),
        lax.all_gather(assignment, "dp", axis=0, tiled=True),
    )
    match_owner = all_owner[None, :] == owned_slots[:, None]
    mine_rows = jnp.dot(
        match_owner.astype(jnp.bfloat16), all_rows, preferred_element_type=jnp.float32
    ).astype(jnp.bfloat16)
    mine_ids = jnp.sum(jnp.where(match_owner, all_ids[None, :], 0), 1).astype(jnp.int32)
    normed_rows = norm_rows(mine_rows.astype(jnp.float32)).astype(jnp.bfloat16)
    logits = jnp.dot(normed_rows, embed.T, preferred_element_type=jnp.float32)
    scored = target_score(logits, mine_ids)
    return (states, logits, scored)

F32 = jnp.float32
BF16 = jnp.bfloat16
VMEM_LIMIT = 60 * 1024 * 1024
SMEM_SPEC = pl.BlockSpec(memory_space=pltpu.SMEM)
HBM_SPEC = pl.BlockSpec(memory_space=pltpu.HBM)


def params(*semantics, limit=VMEM_LIMIT):
    return pltpu.CompilerParams(
        vmem_limit_bytes=limit, dimension_semantics=semantics or None
    )


def norm_kernel(column_ref, picked_ref, x_ref, out_ref, rows_ref):
    blocks, size, width = x_ref.shape
    count = blocks * width
    base = pl.program_id(0) * size
    slot = lax.broadcasted_iota(jnp.int32, (rows_ref.shape[1], size), 0)
    row = lax.broadcasted_iota(jnp.int32, (rows_ref.shape[1], size), 1) + base
    hit = sum(
        ((slot == j) & (row == picked_ref[j])).astype(F32) for j in range(picked_ref.shape[0])
    ).astype(BF16)

    @pl.when(pl.program_id(0) == 0)
    def _():
        rows_ref[...] = jnp.zeros_like(rows_ref)

    for b in range(blocks):
        rows_ref[b ^ column_ref[0]] += jnp.dot(hit, x_ref[b], preferred_element_type=F32)
    values = [x_ref[b].astype(F32) for b in range(blocks)]
    average = sum(jnp.sum(v, -1, keepdims=True) for v in values) / count
    centred = [v - average for v in values]
    spread = sum(jnp.sum(v * v, -1, keepdims=True) for v in centred) / count
    scale = lax.rsqrt(spread + EPSILON)
    for b in range(blocks):
        out_ref[:, b * width : (b + 1) * width] = (centred[b] * scale).astype(BF16)


def norm_blocks(column, picked, stack, row_block=224):
    blocks, rows, width = stack.shape
    return pl.pallas_call(
        norm_kernel,
        grid=(rows // row_block,),
        in_specs=[
            SMEM_SPEC,
            SMEM_SPEC,
            pl.BlockSpec((blocks, row_block, width), lambda i: (0, i, 0)),
        ],
        out_specs=[
            pl.BlockSpec((row_block, blocks * width), lambda i: (i, 0)),
            pl.BlockSpec((blocks, 8, width), lambda i: (0, 0, 0)),
        ],
        out_shape=[
            jax.ShapeDtypeStruct((rows, blocks * width), BF16),
            jax.ShapeDtypeStruct((blocks, 8, width), F32),
        ],
        compiler_params=params("arbitrary"),
        cost_estimate=pl.CostEstimate(
            flops=8 * stack.size, bytes_accessed=4 * stack.size, transcendentals=rows
        ),
        name="norm_rows",
    )(column[None].astype(jnp.int32), picked, stack)


def shard_parts(part, shard, half):
    if len(shard) == 2:
        mine, other = shard
        return [
            (mine, pl.multiple_of(part * half, half)),
            (other, pl.multiple_of((1 - part) * half, half)),
        ]
    return [(shard[0].at[pl.ds(j * half, half)], j * half) for j in range(2)]


def take_shards(refs, lengths):
    return [tuple(refs.pop(0) for _ in range(n)) for n in lengths]


def project_kernel(scale, rotated, lengths, place_ref, x_ref, *refs):
    refs = list(refs)
    shards = take_shards(refs, lengths)
    if rotated:
        cos, sin = refs.pop(0)[...], refs.pop(0)[...]
    out_ref, wbuf, sems = refs
    depth, width = shards[0][0].shape
    half = depth // 2

    @pl.when(pl.program_id(0) == 0)
    def _():
        copies = []
        for k, shard in enumerate(shards):
            for j, (source, row) in enumerate(shard_parts(place_ref[0], shard, half)):
                row = pl.multiple_of(place_ref[1 + k] * depth + row, half)
                copies.append(
                    pltpu.make_async_copy(source, wbuf.at[pl.ds(row, half)], sems.at[k, j])
                )
        for copy in copies:
            copy.start()
        for copy in copies:
            copy.wait()

    total = jnp.dot(x_ref[...], wbuf[...], preferred_element_type=F32)
    if not rotated:
        out_ref[...] = total.astype(BF16)
        return
    if scale is not None:
        total = total * scale
    for h in range(width // HS):
        field = total[:, h * HS : (h + 1) * HS]
        turned = pltpu.roll(field, HS // 2, 1)
        out_ref[:, h * HS : (h + 1) * HS] = (field * cos + turned * sin).astype(BF16)


def project(place, normed, shards, scale=None, turn=(), row_block=448):
    rows, features = normed.shape
    width = shards[0][0].shape[1]
    flat = [ref for shard in shards for ref in shard]
    in_specs = [SMEM_SPEC, pl.BlockSpec((row_block, features), lambda i: (i, 0))]
    in_specs += [HBM_SPEC] * len(flat)
    in_specs += [pl.BlockSpec((row_block, HS), lambda i: (i, 0)) for _ in turn]
    return pl.pallas_call(
        functools.partial(
            project_kernel, scale, bool(turn), [len(shard) for shard in shards]
        ),
        grid=(rows // row_block,),
        in_specs=in_specs,
        out_specs=pl.BlockSpec((row_block, width), lambda i: (i, 0)),
        out_shape=jax.ShapeDtypeStruct((rows, width), BF16),
        scratch_shapes=[
            pltpu.VMEM((features, width), BF16),
            pltpu.SemaphoreType.DMA((4, 2)),
        ],
        compiler_params=params("arbitrary"),
        cost_estimate=pl.CostEstimate(
            flops=2 * rows * features * width,
            bytes_accessed=2 * (normed.size + (features + rows) * width),
            transcendentals=0,
        ),
        name="project",
    )(place, normed, *flat, *turn)


def attend_rows(base, ends_ref, q_ref, k_ref, v_ref, out_ref):
    size, count = q_ref.shape[0], k_ref.shape[0]
    sequences = ends_ref.shape[0]
    col = lax.broadcasted_iota(jnp.int32, (1, count), 1)
    col_label = sum((col >= ends_ref[j]).astype(jnp.int32) for j in range(sequences - 1))
    row = lax.broadcasted_iota(jnp.int32, (size, 1), 0) + base
    row_label = sum((row >= ends_ref[j]).astype(jnp.int32) for j in range(sequences - 1))
    for h in range(q_ref.shape[1] // HS):
        head = slice(h * HS, (h + 1) * HS)
        scores = lax.dot_general(
            q_ref[:, head],
            k_ref[:, head],
            (((1,), (1,)), ((), ())),
            preferred_element_type=F32,
        )
        scores = jnp.where(row_label == col_label, scores, -1e30)
        top = jnp.max(scores, -1, keepdims=True)
        raised = jnp.exp(scores - top)
        weights = raised * (1.0 / jnp.sum(raised, -1, keepdims=True))
        out_ref[:, head] = jnp.dot(
            weights.astype(BF16), v_ref[:, head], preferred_element_type=F32
        ).astype(BF16)


def attend_kernel(place_ref, ends_ref, q_ref, k_ref, v_ref, out_ref):
    base = place_ref[1] * q_ref.shape[0]
    attend_rows(base, ends_ref, q_ref, k_ref, v_ref, out_ref)


def value_attend_kernel(lengths, place_ref, half_ref, ends_ref, x_ref, q_ref, k_ref, *refs):
    refs = list(refs)
    shards = take_shards(refs, lengths)
    value_ref, out_ref, wbuf, xbuf, qbuf, kbuf, vbuf, w_sems, sems = refs
    depth = shards[0][0].shape[0]
    half = depth // 2
    copies = [pltpu.make_async_copy(x_ref, xbuf, sems.at[0])]
    for k, shard in enumerate(shards):
        for j, (source, row) in enumerate(shard_parts(place_ref[0], shard, half)):
            row = pl.multiple_of(place_ref[1 + k] * depth + row, half)
            copies.append(
                pltpu.make_async_copy(source, wbuf.at[pl.ds(row, half)], w_sems.at[k, j])
            )
    size = qbuf.shape[0]
    base = pl.multiple_of(half_ref[1] * size, size)
    later = [
        pltpu.make_async_copy(k_ref, kbuf, sems.at[1]),
        pltpu.make_async_copy(q_ref.at[pl.ds(base, size)], qbuf, sems.at[2]),
    ]
    for copy in copies + later:
        copy.start()
    for copy in copies:
        copy.wait()
    vbuf[...] = jnp.dot(xbuf[...], wbuf[...], preferred_element_type=F32).astype(BF16)
    store = pltpu.make_async_copy(vbuf, value_ref, sems.at[3])
    store.start()
    for copy in later:
        copy.wait()
    attend_rows(base, ends_ref, qbuf, kbuf, vbuf, out_ref)
    store.wait()


def value_attend(place, half_place, ends, normed, queries, key_rows, shards):
    rows, features = normed.shape
    columns = queries.shape[1]
    half = rows // 2
    flat = [ref for shard in shards for ref in shard]
    return pl.pallas_call(
        functools.partial(value_attend_kernel, [len(shard) for shard in shards]),
        in_specs=[SMEM_SPEC] * 3 + [HBM_SPEC] * (3 + len(flat)),
        out_specs=[HBM_SPEC, pl.BlockSpec(memory_space=pltpu.VMEM)],
        out_shape=[
            jax.ShapeDtypeStruct((rows, columns), BF16),
            jax.ShapeDtypeStruct((half, columns), BF16),
        ],
        scratch_shapes=[
            pltpu.VMEM((features, columns), BF16),
            pltpu.VMEM((rows, features), BF16),
            pltpu.VMEM((half, columns), BF16),
            pltpu.VMEM((rows, columns), BF16),
            pltpu.VMEM((rows, columns), BF16),
            pltpu.SemaphoreType.DMA((4, 2)),
            pltpu.SemaphoreType.DMA((4,)),
        ],
        compiler_params=params(),
        cost_estimate=pl.CostEstimate(
            flops=2 * rows * columns * (features + rows),
            bytes_accessed=2 * (normed.size + (features + 4 * rows) * columns),
            transcendentals=half * rows * columns // HS,
        ),
        name="value_attend",
    )(place, half_place, ends, normed, queries, key_rows, *flat)


def attention(place, ends, queries, key_rows, value_rows):
    rows, columns = queries.shape
    half = rows // 2
    heads = columns // HS
    return pl.pallas_call(
        attend_kernel,
        grid_spec=pltpu.PrefetchScalarGridSpec(
            num_scalar_prefetch=2,
            grid=(1,),
            in_specs=[
                pl.BlockSpec((half, columns), lambda h, place, ends: (place[1], h)),
                pl.BlockSpec((rows, columns), lambda h, place, ends: (0, h)),
                pl.BlockSpec((rows, columns), lambda h, place, ends: (0, h)),
            ],
            out_specs=pl.BlockSpec((half, columns), lambda h, place, ends: (0, h)),
        ),
        out_shape=jax.ShapeDtypeStruct((half, columns), BF16),
        compiler_params=params("arbitrary"),
        cost_estimate=pl.CostEstimate(
            flops=4 * half * rows * columns,
            bytes_accessed=6 * rows * columns,
            transcendentals=half * rows * heads,
        ),
        name="attention",
    )(place, ends, queries, key_rows, value_rows)


def out_kernel(adding, base, lengths, place_ref, *refs):
    refs = list(refs)
    if adding:
        x_ref, come_ref = refs.pop(0), refs.pop(0)
    else:
        picked_ref, x_ref, kept_ref = refs.pop(0), refs.pop(0), refs.pop(0)
    shards = take_shards(refs, lengths)
    out_ref = refs.pop(0)
    if not adding:
        rows_ref, marked = refs.pop(0), refs.pop()
    wbuf, sems = refs
    block = pl.program_id(0)
    half = wbuf.shape[1] // 2
    part, core = place_ref[0], place_ref[5]

    @pl.when(block == 0)
    def _():
        for k, shard in enumerate(shards):
            spot = place_ref[1 + k] - base

            @pl.when((spot >= 0) & (spot < 2))
            def _():
                for j, (source, row) in enumerate(shard_parts(part, shard, half)):
                    pltpu.make_async_copy(
                        source, wbuf.at[spot, pl.ds(row, half)], sems.at[spot, j]
                    ).start()

        if not adding:
            size = x_ref.shape[0]
            slot = lax.broadcasted_iota(jnp.int32, (marked.shape[0], size), 0)
            row = lax.broadcasted_iota(jnp.int32, (marked.shape[0], size), 1)
            total = None
            for ref, first in ((x_ref, (1 - core) * size), (kept_ref, core * size)):
                hit = sum(
                    ((slot == j) & (row + first == picked_ref[j])).astype(F32)
                    for j in range(picked_ref.shape[0])
                )
                term = jnp.dot(hit.astype(BF16), ref[...], preferred_element_type=F32)
                total = term if total is None else total + term
            marked[...] = total.astype(BF16)

    for j in range(2):
        pltpu.make_async_copy(
            shards[0][0].at[pl.ds(0, half)],
            wbuf.at[block, pl.ds(j * half, half)],
            sems.at[block, j],
        ).wait()
    total = jnp.dot(x_ref[...], wbuf[block], preferred_element_type=F32)
    if adding:
        total = total + come_ref[...].astype(F32)
    else:
        rows_ref[...] = jnp.dot(marked[...], wbuf[block], preferred_element_type=F32)
    out_ref[...] = total.astype(BF16)


def out_project(place, context, shards, base, come=None, picked=None, kept=None):
    half, depth = context.shape
    width = shards[0][0].shape[1]
    flat = [ref for shard in shards for ref in shard]
    adding = come is not None
    whole = pl.BlockSpec((half, depth), lambda j: (0, 0))
    if adding:
        operands = [place, context, come]
        in_specs = [SMEM_SPEC, whole]
        in_specs += [pl.BlockSpec((None, half, width), lambda j: (1 - j, 0, 0))]
    else:
        operands = [place, picked, context, kept]
        in_specs = [SMEM_SPEC, SMEM_SPEC, whole, whole]
    out_specs = [pl.BlockSpec((None, half, width), lambda j: (j, 0, 0))]
    out_shape = [jax.ShapeDtypeStruct((2, half, width), BF16)]
    scratch = [pltpu.VMEM((2, depth, width), BF16), pltpu.SemaphoreType.DMA((2, 2))]
    if not adding:
        out_specs.append(pl.BlockSpec((None, 8, width), lambda j: (j, 0, 0)))
        out_shape.append(jax.ShapeDtypeStruct((2, 8, width), F32))
        scratch.append(pltpu.VMEM((8, depth), BF16))
    return pl.pallas_call(
        functools.partial(out_kernel, adding, base, [len(shard) for shard in shards]),
        grid=(2,),
        in_specs=in_specs + [HBM_SPEC] * len(flat),
        out_specs=out_specs,
        out_shape=out_shape,
        scratch_shapes=scratch,
        compiler_params=params("arbitrary", limit=24 * 1024 * 1024),
        cost_estimate=pl.CostEstimate(
            flops=4 * half * depth * width,
            bytes_accessed=2 * (half * depth + 2 * (depth + (1 + adding) * half) * width),
            transcendentals=0,
        ),
        name="out_project",
    )(*operands, *flat)


def tie(value, *earlier):
    return lax.optimization_barrier((value, *earlier))[0]


class WeightRing:
    def __init__(self, dp):
        self.dp = dp
        self.part = lax.axis_index("parts")
        self.along, self.across, self.shards = [], [], []

    def ring(self, value, step):
        return lax.ppermute(value, "dp", [(i, (i + step) % self.dp) for i in range(self.dp)])

    def step(self, value, step, before=(), before_swap=(), gather=False):
        i = len(self.along)
        waits = list(before) + self.along[i - 2 : i - 1] if i >= 2 else list(before)
        self.along.append(self.ring(tie(value, *waits), step))
        if gather:
            whole = lax.all_gather(self.along[i], "parts", axis=0, tiled=True)
            self.shards.append((whole,))
            return
        waits = self.across[-2:-1]
        self.across.append(
            lax.ppermute(tie(self.along[i], *waits, *before_swap), "parts", [(0, 1), (1, 0)])
        )
        self.shards.append((self.along[i], self.across[-1]))

    def half(self, weight):
        size = weight.shape[0] // 2
        return lax.dynamic_slice_in_dim(weight, self.part * size, size, 0)

    def pieces(self, group):
        first = 3 * group
        return [self.shards[i] for i in (first, first + 2, first + 1)]


def per_device(
    hidden, lengths, mask_pos, token_ids, assignment, w_query, w_key, w_value, w_out, embed
):
    dp, fsdp = 4, 4
    rows, width = hidden.shape
    half = rows // 2
    sequences = lengths.shape[0]
    part = lax.axis_index("parts")
    group = lax.axis_index("dp")
    column = lax.axis_index("fsdp")
    core = column % 2
    ring_order = [lax.rem(group + dp - k, dp) for k in range(dp)]
    place = jnp.stack([part] + ring_order).astype(jnp.int32)
    stack = lax.all_gather(hidden, "fsdp", axis=0, tiled=False)
    segment, position, starts = layout(lengths, rows)
    half_width = HS // 2
    frequency = 10000.0 ** (-2.0 * jnp.arange(half_width, dtype=F32) / HS)
    angles = position.astype(F32)[:, None] * frequency[None, :]
    sine, cosine = jnp.sin(angles), jnp.cos(angles)
    turn = (jnp.concatenate([cosine, cosine], -1), jnp.concatenate([-sine, sine], -1))
    picked = starts + mask_pos
    chosen = jnp.arange(rows, dtype=jnp.int32)[None, :] == picked[:, None]
    local_ids = jnp.sum(jnp.where(chosen, token_ids[None, :], 0), 1)

    ends = jnp.cumsum(lengths)
    keep_place = jnp.stack([part, core]).astype(jnp.int32)
    send_place = jnp.stack([part, 1 - core]).astype(jnp.int32)
    out_place = jnp.stack([part] + [s ^ column for s in ring_order] + [core]).astype(jnp.int32)

    def swap_by(value, mask):
        return lax.ppermute(value, "fsdp", [(i, i ^ mask) for i in range(fsdp)])

    def by_offset(blocks):
        return jnp.stack(
            [
                lax.dynamic_index_in_dim(blocks, column ^ r, 0, keepdims=False)
                for r in range(fsdp)
            ]
        )

    extra = jnp.stack([local_ids, assignment], 1).astype(BF16)
    extra = jnp.pad(extra, ((0, 8 - sequences), (0, width - 2)))[None]

    ring = WeightRing(dp)
    mine = ring.half(w_key)
    ring.step(mine, 1)
    ring.step(mine, -1)
    ring.step(ring.along[0], 1)
    mine = ring.half(w_query)
    ring.step(mine, 1)
    ring.step(mine, -1)
    normed, hidden_rows = norm_blocks(column, picked, stack)
    ring.step(ring.along[3], 1)
    key_rows = project(place, normed, [(w_key,), *ring.pieces(0)], None, turn)
    mine = ring.half(w_value)
    ring.step(mine, 1, before=[normed])
    queries = project(place, normed, [(w_query,), *ring.pieces(1)], HS ** (-0.5), turn)
    ring.step(mine, -1, before=[key_rows], before_swap=[queries])
    ring.step(ring.along[6], 1)
    mine = ring.half(w_out)
    ring.step(mine, 1)
    value_rows, context_sent = value_attend(
        place, send_place, ends, normed, queries, key_rows, [(w_value,), *ring.pieces(2)]
    )
    ring.step(mine, -1, before=[queries], before_swap=[context_sent])
    last_along = ring.ring(tie(ring.along[9], ring.along[9]), 1)
    last_other = ring.ring(tie(ring.across[-2], ring.along[10], context_sent), 1)
    out_in = [(w_out,), ring.shards[9], (last_along, last_other), ring.shards[10]]
    context_kept = attention(keep_place, ends, queries, key_rows, tie(value_rows, context_sent))

    def send(base, *before):
        return out_project(
            out_place, tie(context_sent, *before), out_in, base, None, picked, context_kept
        )

    sent_far, rows_far = send(2)
    arrived_far = swap_by(sent_far, 1)
    sent_near, rows_near = send(0, sent_far)
    arrived_near = swap_by(sent_near, 1)
    (chip_far,) = out_project(
        out_place, tie(context_kept, sent_near), out_in, 2, arrived_far
    )
    crossed = swap_by(chip_far, 2)
    (chip_near,) = out_project(
        out_place, tie(context_kept, chip_far), out_in, 0, arrived_near
    )

    own_sum = jnp.concatenate([rows_near, rows_far], 0)
    row_sum = own_sum
    for mask in range(1, fsdp):
        come = swap_by(own_sum, mask)
        row_sum = row_sum + jnp.stack([come[r ^ mask] for r in range(fsdp)])
    full_rows = (hidden_rows + row_sum).astype(BF16)
    packet = jnp.concatenate([full_rows, extra], 0)
    packets = [packet] + [ring.ring(packet, shift) for shift in range(1, dp)]
    packets = tie(jnp.stack(packets), crossed)[:, :, :sequences]
    all_rows = by_offset(packets[:, :dp].transpose(1, 0, 2, 3).reshape(dp, dp * sequences, width))
    all_rows = all_rows.transpose(1, 0, 2).reshape(dp * sequences, dp * width)
    all_ids = packets[:, dp, :, 0].reshape(-1).astype(jnp.int32)
    all_owner = packets[:, dp, :, 1].reshape(-1).astype(jnp.int32)
    owned = group * sequences + jnp.arange(sequences, dtype=jnp.int32)
    match = all_owner[None, :] == owned[:, None]
    mine_rows = jnp.dot(match.astype(BF16), all_rows, preferred_element_type=F32)
    mine_ids = jnp.sum(jnp.where(match, all_ids[None, :], 0), 1).astype(jnp.int32)
    normed_rows = norm_rows(mine_rows).astype(BF16)
    logits = jnp.dot(normed_rows, embed.T, preferred_element_type=F32)
    scored = target_score(logits, mine_ids)

    def block_rows(index, place_in_chip):
        before = lax.dynamic_slice(stack, (index, core * half, 0), (1, half, width))[0]
        summed = chip_near[place_in_chip].astype(F32) + crossed[place_in_chip].astype(F32)
        return (before.astype(F32) + summed).astype(BF16)

    other_rows = swap_by(block_rows(column ^ 1, 1), 1)
    own_rows = block_rows(column, 0)
    states = jnp.where(
        core == 0,
        jnp.concatenate([own_rows, other_rows], 0),
        jnp.concatenate([other_rows, own_rows], 0),
    )
    return (states, logits, scored)


def ring_fits(mesh):
    return (mesh.shape["parts"], mesh.shape["dp"], mesh.shape["fsdp"]) == (2, 4, 4)


def solution(mesh):
    return jax.shard_map(
        per_device if ring_fits(mesh) else per_device_any,
        mesh=mesh,
        in_specs=(
            P(("parts", "dp"), "fsdp"),
            P(("parts", "dp")),
            P(("parts", "dp")),
            P(("parts", "dp")),
            P(("parts", "dp")),
            P("dp", "fsdp"),
            P("dp", "fsdp"),
            P("dp", "fsdp"),
            P("fsdp", "dp"),
            P(),
        ),
        out_specs=(P(("parts", "dp"), "fsdp"), P(("parts", "dp"), None), P(("parts", "dp"))),
        check_vma=False,
    )
```
